256 devices in a mesh: mesh: 128 (over x_lo, z, y, core), band: 2 (over x_hi).
Axes of the slice: x: 4 (x_hi: 2, x_lo: 2; x = x_hi * 2 + x_lo), y: 4, z: 8, core: 2. Of those that a mesh axis runs over, the one named last changes fastest.
Arguments:
- states: float32 [110592, 512], P('mesh', 'band'), may hold values from -6 to 6
- inv_sqrt_mass: float32 [110592], P('mesh'), may hold values from 0.7 to 1.3
- stiffness: float32 [343, 343], replicated, as said below
- cell_scale: float32 [512], P('mesh'), may hold values from 0.5 to 2
- potential: float32 [512, 343], P('mesh'), may hold values from -1 to 1
- connectivity: int32 [512, 343], P('mesh'), may hold values from 0 to 1295
- shared_rows: int32 [128, 2, 216], P('mesh'), may hold values from 0 to 863
- coefficients: float32 [512, 512], P('band'), may hold values from -0.25 to 0.25
Outputs:
- rotated: float32 [110592, 512], P('mesh', 'band')
The draws below stay inside these ranges and needn't reach their ends.
Inputs may be any that keep to these rules, and one draw needn't show every extreme that they name: stiffness is symmetric.
All inputs are finite; a program needn't handle non-finite values.
Results may differ from the reference program's by a relative error of at most 0.0001.
Values sent between devices are 32-bit elements; how exact they have to be, the bound alone decides.
A program may use at most 64 MiB of HBM per device.

```python
import math
import jax
import jax.numpy as jnp
from jax import lax

NPE = 343
DEGREE = 3
CELLS_DEV = 4
NODE_DEV = 864
GHOST = 216
NODES = 110592
CELLS = 512
NST = 512
N_MESH = 128


def draw_stiffness(key, part):
    key = jax.random.fold_in(key, 11)
    entries = jax.random.normal(key, (NPE, NPE), jnp.float32) * NPE ** (-0.5)
    return 0.5 * (entries + entries.T) + 2.0 * jnp.eye(NPE, dtype=jnp.float32)


def touch_ends(drawn, key, least, high):
    extent = drawn.shape
    index_at = [jax.random.randint(jax.random.fold_in(key, axis), (), 0, extent[axis]) for axis in range(len(extent))]
    drawn = drawn.at[tuple(index_at)].set(least)
    longest = extent.index(max(extent))
    index_at[longest] = (index_at[longest] + 1) % extent[longest]
    return drawn.at[tuple(index_at)].set(high)


def steps_of(rng, shape, cuts, low, largest):
    def one(axis_at, blocks):
        steps = jax.random.uniform(jax.random.fold_in(jax.random.fold_in(rng, 6), axis_at), (blocks,), jnp.float32, low / len(cuts), largest / len(cuts))
        return jnp.repeat(jnp.exp(steps), shape[axis_at] // blocks).reshape((-1,) + (1,) * (len(shape) - axis_at - 1))

    level = one(*cuts[0])
    for cut in cuts[1:]:
        level = level * one(*cut)
    return level


def centred(key, shape, spread, limit, split=(), held_as=jnp.bfloat16):
    factor_of = steps_of(key, shape, split, -0.22, 0.18) if split else 1.0
    drawn = jax.random.normal(key, shape, jnp.float32) * spread * factor_of
    return jnp.minimum(jnp.maximum(drawn, -limit), limit).astype(held_as)


def setup_inputs(seed: int = 0) -> dict:
    key_of = jax.random.split(jax.random.key(seed), 9)
    states = centred(key_of[0], (NODES, NST), 1.0, 6.0, ((0, 128), (1, 2)), jnp.float32)
    inv_sqrt_mass = jnp.clip(jnp.exp(math.log(1.3) - 0.6190392 * jax.random.uniform(key_of[1], (NODES,), jnp.float32) ** steps_of(key_of[1], (NODES,), ((0, 128),), -0.2, 0.2)), 0.7, 1.3)
    stiffness = draw_stiffness(jax.random.fold_in(key_of[8], 71), 0)
    cell_scale = jnp.clip(jnp.exp(math.log(2.0) - 1.3862944 * jax.random.uniform(key_of[3], (CELLS,), jnp.float32) ** steps_of(key_of[3], (CELLS,), ((0, 128),), -0.2, 0.2)), 0.5, 2.0)
    potential = jnp.clip(jax.random.uniform(key_of[4], (CELLS, NPE), jnp.float32, -1.0, 1.0) * steps_of(key_of[4], (CELLS, NPE), ((0, 128),), -0.4, 0.0), -1.0, 1.0)
    connectivity = touch_ends(jax.random.randint(key_of[5], (CELLS, NPE), 0, NODE_DEV + 2 * GHOST), jax.random.fold_in(key_of[5], 1), 0, (NODE_DEV + 2 * GHOST) - 1).astype(jnp.int32)
    shared_rows = touch_ends(jax.random.randint(key_of[6], (N_MESH, 2, GHOST), 0, NODE_DEV), jax.random.fold_in(key_of[6], 1), 0, NODE_DEV - 1).astype(jnp.int32)
    coefficients = centred(key_of[7], (NST, NST), NST ** -0.5, 0.25, ((0, 2),), jnp.float32)
    return dict(states=states, inv_sqrt_mass=inv_sqrt_mass, stiffness=stiffness, cell_scale=cell_scale, potential=potential, connectivity=connectivity, shared_rows=shared_rows, coefficients=coefficients)


low_end = -3.0
low_bound = 2.0
high_bound = 14.0

def node_map(connectivity, shared_rows):
    partition = (jnp.arange(CELLS, dtype=jnp.int32) // CELLS_DEV)[:, None]
    node_slot = connectivity
    own_global = partition * NODE_DEV + node_slot
    lower_part = jnp.clip(partition - 1, 0, N_MESH - 1)
    upper_part = jnp.clip(partition + 1, 0, N_MESH - 1)
    lower_slot = jnp.clip(node_slot - NODE_DEV, 0, GHOST - 1)
    upper_slot = jnp.clip(node_slot - NODE_DEV - GHOST, 0, GHOST - 1)
    lower_node = jnp.where(partition > 0, lower_part * NODE_DEV + shared_rows[lower_part, 1, lower_slot], NODES)
    upper_node = jnp.where(partition < N_MESH - 1, upper_part * NODE_DEV + shared_rows[upper_part, 0, upper_slot], NODES)
    result = jnp.where(node_slot < NODE_DEV, own_global, jnp.where(node_slot < NODE_DEV + GHOST, lower_node, upper_node))
    return result.astype(jnp.int32)

def reference(states, inv_sqrt_mass, stiffness, cell_scale, potential, connectivity, shared_rows, coefficients):
    global_nodes = node_map(connectivity, shared_rows)
    flat_nodes = global_nodes.reshape(-1)

    def apply_operator(values_in):
        block_width = values_in.shape[1]
        scaled = inv_sqrt_mass[:, None] * values_in
        padded = jnp.concatenate([scaled, jnp.zeros((1, block_width), jnp.float32)], axis=0)
        gathered = padded[global_nodes]
        cell_terms = cell_scale[:, None, None] * jnp.einsum('ij,cjs->cis', stiffness, gathered, precision=lax.Precision.HIGHEST) + potential[:, :, None] * gathered
        summed = jnp.zeros((NODES + 1, block_width), jnp.float32).at[flat_nodes].add(cell_terms.reshape(-1, block_width))
        return inv_sqrt_mass[:, None] * summed[:NODES]
    half_span = (high_bound - low_bound) / 2.0
    centre = (high_bound + low_bound) / 2.0
    sigma_first = half_span / (low_end - centre)
    gamma_term = 2.0 / sigma_first

    def filter_block(block_states):
        current = (apply_operator(block_states) - centre * block_states) * (sigma_first / half_span)
        previous = block_states
        sigma_now = sigma_first
        for step_index in range(DEGREE - 1):
            sigma_next = 1.0 / (gamma_term - sigma_now)
            following = (apply_operator(current) - centre * current) * (2.0 * sigma_next / half_span) - sigma_now * sigma_next * previous
            previous = current
            current = following
            sigma_now = sigma_next
        return current
    block_count = NST // 64
    blocks = states.reshape(NODES, block_count, 64).transpose(1, 0, 2)
    filtered = lax.map(filter_block, blocks).transpose(1, 0, 2).reshape(NODES, NST)
    return jnp.dot(filtered, coefficients, precision=lax.Precision.HIGHEST, preferred_element_type=jnp.float32)
```

```python
import jax
import jax.numpy as jnp
from jax import lax
from jax.experimental import pallas as pl
from jax.experimental.pallas import tpu as pltpu
from jax.sharding import PartitionSpec as P

MESH = pl.DeviceIdType.MESH
F32, BF16 = jnp.float32, jnp.bfloat16

DEGREE = 3
OWN = 864
GHOST = 216
NODES = OWN + 2 * GHOST
NPE = 343
PAD = 384
CELLS = 4
W = 128
BANDW = 256

low_end = -3.0
low_bound = 2.0
high_bound = 14.0

half_span = (high_bound - low_bound) / 2.0
centre = (high_bound + low_bound) / 2.0
sigma_first = half_span / (low_end - centre)
gamma_term = 2.0 / sigma_first


def chebyshev():
    rows = [(sigma_first / half_span, 0.0)]
    now = sigma_first
    for _ in range(DEGREE - 1):
        later = 1.0 / (gamma_term - now)
        rows.append((2.0 * later / half_span, now * later))
        now = later
    return rows


COEFS = chebyshev()


def dot(a, b):
    return jnp.dot(a, b, preferred_element_type=F32)


def dot_nt(a, b):
    return lax.dot_general(a, b, (((1,), (1,)), ((), ())), preferred_element_type=F32)


def split(x):
    high = x.astype(BF16)
    return high, (x - high.astype(F32)).astype(BF16)


def pair(x):
    return jnp.concatenate(split(x), axis=1)


def fold(y):
    return y[:, :W] + y[:, W:]


def apply_pair(high, low, packed):
    return fold(dot(high, packed)) + dot(low, packed[:, :W])


def kernel(
    parts,
    states,
    mass,
    stiffness,
    scale,
    potential,
    slots,
    shared,
    coefficients,
    out,
    stiff_pad,
    slot_pad,
    pot_pad,
    turn,
    mass_cols,
    one_hot,
    prod_own_hi,
    prod_own_lo,
    prod_ghost_hi,
    prod_ghost_lo,
    own_hi,
    own_lo,
    ghost_hi,
    ghost_lo,
    pick,
    place,
    band_out,
    band_in,
    value,
    before,
    pre,
    acc,
    ghost_out,
    ghost_in,
    back_out,
    back_in,
    band_send,
    band_recv,
    ghost_send,
    ghost_recv,
    back_send,
    back_recv,
):
    me = lax.axis_index("mesh")
    band = lax.axis_index("band")
    lower = (lax.rem(me + parts - 1, parts), band)
    upper = (lax.rem(me + 1, parts), band)
    other = (me, 1 - band)

    barrier = pltpu.get_barrier_semaphore()
    for device in (other, lower, upper):
        pl.semaphore_signal(barrier, inc=1, device_id=device, device_id_type=MESH)

    def band_copy(j):
        return pltpu.make_async_remote_copy(
            src_ref=band_out.at[j],
            dst_ref=band_in.at[j],
            send_sem=band_send.at[j],
            recv_sem=band_recv.at[j],
            device_id=other,
            device_id_type=MESH,
        )

    def chain_copies(src, dst, send, recv, k, j):
        down = pltpu.make_async_remote_copy(
            src_ref=src.at[k, j, pl.ds(0, GHOST)],
            dst_ref=dst.at[k, j, pl.ds(GHOST, GHOST)],
            send_sem=send.at[k, j, 0],
            recv_sem=recv.at[k, j, 0],
            device_id=lower,
            device_id_type=MESH,
        )
        up = pltpu.make_async_remote_copy(
            src_ref=src.at[k, j, pl.ds(GHOST, GHOST)],
            dst_ref=dst.at[k, j, pl.ds(0, GHOST)],
            send_sem=send.at[k, j, 1],
            recv_sem=recv.at[k, j, 1],
            device_id=upper,
            device_id_type=MESH,
        )
        return down, up

    def ghost_copies(k, j):
        return chain_copies(ghost_out, ghost_in, ghost_send, ghost_recv, k, j)

    def back_copies(k, j):
        return chain_copies(back_out, back_in, back_send, back_recv, k, j)

    x_hi, x_lo = split(states[...])

    def rotated_chunk(which, j):
        at = pl.multiple_of(which * BANDW + j * W, W)
        c_hi, c_lo = split(coefficients[:, pl.ds(at, W)])
        return fold(dot(x_hi, jnp.concatenate([c_hi, c_lo], axis=1))) + dot(x_lo, c_hi)

    for j in range(2):
        band_out[j] = rotated_chunk(1 - band, j)
        if j == 0:
            pl.semaphore_wait(barrier, 3)
        band_copy(j).start()
    for j in range(2):
        value[j] = rotated_chunk(band, j)

    turn[...] = jnp.zeros_like(turn)
    turn[:, :OWN] = jnp.broadcast_to(mass[...], (W, OWN))
    mass_cols[...] = turn[...].T[:OWN]

    rows = shared[...]
    place[...] = jnp.where(
        lax.broadcasted_iota(jnp.int32, (OWN, 2 * GHOST), 0) == rows, 1.0, 0.0
    ).astype(BF16)
    turn[:, : 2 * GHOST] = jnp.broadcast_to(rows.astype(F32), (W, 2 * GHOST))
    columns = turn[:, :512].T[: 2 * GHOST].astype(jnp.int32)
    for at in range(0, OWN, W):
        width = min(W, OWN - at)
        pick[:, at : at + width] = jnp.where(
            lax.broadcasted_iota(jnp.int32, (2 * GHOST, width), 1) + at == columns[:, :width],
            1.0,
            0.0,
        ).astype(BF16)

    stiff_pad[...] = jnp.zeros_like(stiff_pad)
    stiff_pad[:NPE, :NPE] = stiffness[...]
    slot_pad[...] = jnp.full(slot_pad.shape, -1, jnp.int32)
    drawn = slots[...]
    absent = ((me == 0) & (drawn >= OWN) & (drawn < OWN + GHOST)) | (
        (me == parts - 1) & (drawn >= OWN + GHOST)
    )
    slot_pad[:CELLS, :NPE] = jnp.where(absent, -1, drawn)
    pot_pad[...] = jnp.zeros_like(pot_pad)
    pot_pad[:CELLS, :NPE] = potential[...]

    @pl.loop(0, CELLS)
    def _(c):
        at = pl.multiple_of(c * PAD, PAD)
        row = slot_pad[pl.ds(c, 1), :]
        hot = jnp.where(
            lax.broadcasted_iota(jnp.int32, (NODES, PAD), 0) == row, 1.0, 0.0
        ).astype(BF16)
        one_hot[:, pl.ds(at, PAD)] = hot
        diagonal = lax.broadcasted_iota(jnp.int32, (PAD, PAD), 0) == lax.broadcasted_iota(
            jnp.int32, (PAD, PAD), 1
        )
        cell = scale[c] * stiff_pad[...] + jnp.where(diagonal, pot_pad[pl.ds(c, 1), :], 0.0)
        stacked = jnp.concatenate(split(cell), axis=0)
        for part, high, low in (
            (hot[:OWN], prod_own_hi, prod_own_lo),
            (hot[OWN:], prod_ghost_hi, prod_ghost_lo),
        ):
            both = dot_nt(stacked, part)
            high[pl.ds(at, PAD), :], low[pl.ds(at, PAD), :] = split(both[:PAD] + both[PAD:])

    for high, low, to_hi, to_lo, length in (
        (prod_own_hi, prod_own_lo, own_hi, own_lo, OWN),
        (prod_ghost_hi, prod_ghost_lo, ghost_hi, ghost_lo, 2 * GHOST),
    ):
        for at in range(0, length, 256):
            cols = slice(at, min(at + 256, length))
            block = dot(one_hot[...], high[:, cols]) + dot(one_hot[...], low[:, cols])
            to_hi[:, cols], to_lo[:, cols] = split(block)

    def scatter_own(k, j):
        packed = pair(mass_cols[...] * value[j])
        ghost_out[k, j] = fold(dot(pick[...], packed))
        for copy in ghost_copies(k, j):
            copy.start()
        pre[j] = apply_pair(own_hi[...], own_lo[...], packed)

    def begin(j):
        band_copy(j).wait_recv()
        value[j] = value[j] + band_in[j]
        before[j] = jnp.zeros((OWN, W), F32)
        scatter_own(0, j)

    def ghost_step(k, j):
        for copy in ghost_copies(k, j):
            copy.wait_recv()
        packed = pair(ghost_in[k, j])
        back_out[k, j] = pre[j, OWN:] + apply_pair(ghost_hi[OWN:], ghost_lo[OWN:], packed)
        for copy in back_copies(k, j):
            copy.start()
        acc[j] = pre[j, :OWN] + apply_pair(ghost_hi[:OWN], ghost_lo[:OWN], packed)

    def back_step(k, j, front, past):
        for copy in back_copies(k, j):
            copy.wait_recv()
        u = mass_cols[...] * (acc[j] + fold(dot(place[...], pair(back_in[k, j]))))
        now = value[j]
        return (u - centre * now) * front - past * before[j], now

    def advance(k, j):
        front = jnp.where(k == 0, COEFS[0][0], COEFS[1][0])
        past = jnp.where(k == 0, COEFS[0][1], COEFS[1][1])
        following, now = back_step(k, j, front, past)
        before[j] = now
        value[j] = following
        scatter_own(k + 1, j)

    begin(0)
    ghost_step(0, 0)
    begin(1)

    @pl.loop(0, DEGREE - 1)
    def _(k):
        advance(k, 0)
        ghost_step(k, 1)
        ghost_step(k + 1, 0)
        advance(k, 1)

    last = DEGREE - 1
    out[:, :W] = back_step(last, 0, *COEFS[last])[0]
    ghost_step(last, 1)
    out[:, W:] = back_step(last, 1, *COEFS[last])[0]

    for j in range(2):
        band_copy(j).wait_send()

    @pl.loop(0, DEGREE)
    def _(k):
        for j in range(2):
            for copy in ghost_copies(k, j) + back_copies(k, j):
                copy.wait_send()


def solution(mesh):
    parts = mesh.shape["mesh"]
    vmem = pl.BlockSpec(memory_space=pltpu.VMEM)
    smem = pl.BlockSpec(memory_space=pltpu.SMEM)
    dma = pltpu.SemaphoreType.DMA

    def body(states, mass, stiffness, scale, potential, slots, shared, coefficients):
        def run(*refs):
            kernel(parts, *refs)

        return pl.pallas_call(
            run,
            out_shape=jax.ShapeDtypeStruct((OWN, BANDW), F32),
            in_specs=[vmem, vmem, vmem, smem, vmem, vmem, vmem, vmem],
            out_specs=vmem,
            scratch_shapes=[
                pltpu.VMEM((PAD, PAD), F32),
                pltpu.VMEM((8, PAD), jnp.int32),
                pltpu.VMEM((8, PAD), F32),
                pltpu.VMEM((W, 896), F32),
                pltpu.VMEM((OWN, W), F32),
                pltpu.VMEM((NODES, CELLS * PAD), BF16),
                pltpu.VMEM((CELLS * PAD, OWN), BF16),
                pltpu.VMEM((CELLS * PAD, OWN), BF16),
                pltpu.VMEM((CELLS * PAD, 2 * GHOST), BF16),
                pltpu.VMEM((CELLS * PAD, 2 * GHOST), BF16),
                pltpu.VMEM((NODES, OWN), BF16),
                pltpu.VMEM((NODES, OWN), BF16),
                pltpu.VMEM((NODES, 2 * GHOST), BF16),
                pltpu.VMEM((NODES, 2 * GHOST), BF16),
                pltpu.VMEM((2 * GHOST, OWN), BF16),
                pltpu.VMEM((OWN, 2 * GHOST), BF16),
                pltpu.VMEM((2, OWN, W), F32),
                pltpu.VMEM((2, OWN, W), F32),
                pltpu.VMEM((2, OWN, W), F32),
                pltpu.VMEM((2, OWN, W), F32),
                pltpu.VMEM((2, NODES, W), F32),
                pltpu.VMEM((2, OWN, W), F32),
                pltpu.VMEM((DEGREE, 2, 2 * GHOST, W), F32),
                pltpu.VMEM((DEGREE, 2, 2 * GHOST, W), F32),
                pltpu.VMEM((DEGREE, 2, 2 * GHOST, W), F32),
                pltpu.VMEM((DEGREE, 2, 2 * GHOST, W), F32),
                dma((2,)),
                dma((2,)),
                dma((DEGREE, 2, 2)),
                dma((DEGREE, 2, 2)),
                dma((DEGREE, 2, 2)),
                dma((DEGREE, 2, 2)),
            ],
            compiler_params=pltpu.CompilerParams(
                collective_id=0, has_side_effects=True, vmem_limit_bytes=56 * 2**20
            ),
        )(
            states,
            mass.reshape(1, OWN),
            stiffness,
            scale,
            potential,
            slots,
            shared.reshape(1, 2 * GHOST),
            coefficients,
        )

    return jax.shard_map(
        body,
        mesh=mesh,
        in_specs=(
            P("mesh", "band"),
            P("mesh"),
            P(),
            P("mesh"),
            P("mesh", None),
            P("mesh", None),
            P("mesh", None, None),
            P("band", None),
        ),
        out_specs=P("mesh", "band"),
        check_vma=False,
    )
```

```python
import jax
import jax.numpy as jnp
from jax import lax
from jax.experimental import pallas as pl
from jax.experimental.pallas import tpu as pltpu
from jax.sharding import PartitionSpec as P

MESH = pl.DeviceIdType.MESH
F32, BF16 = jnp.float32, jnp.bfloat16

DEGREE = 3
OWN = 864
GHOST = 216
NODES = OWN + 2 * GHOST
NPE = 343
PAD = 384
CELLS = 4
W = 128
BANDW = 256

low_end = -3.0
low_bound = 2.0
high_bound = 14.0

half_span = (high_bound - low_bound) / 2.0
centre = (high_bound + low_bound) / 2.0
sigma_first = half_span / (low_end - centre)
gamma_term = 2.0 / sigma_first


def chebyshev():
    rows = [(sigma_first / half_span, 0.0)]
    now = sigma_first
    for _ in range(DEGREE - 1):
        later = 1.0 / (gamma_term - now)
        rows.append((2.0 * later / half_span, now * later))
        now = later
    return rows


COEFS = chebyshev()


def dot(a, b):
    return jnp.dot(a, b, preferred_element_type=F32)


def dot_nt(a, b):
    return lax.dot_general(a, b, (((1,), (1,)), ((), ())), preferred_element_type=F32)


def split(x):
    high = x.astype(BF16)
    return high, (x - high.astype(F32)).astype(BF16)


def pair(x):
    return jnp.concatenate(split(x), axis=1)


def fold(y):
    return y[:, :W] + y[:, W:]


def apply_pair(high, low, packed):
    return fold(dot(high, packed)) + dot(low, packed[:, :W])


def kernel(
    parts,
    states,
    mass,
    stiffness,
    scale,
    potential,
    slots,
    shared,
    coefficients,
    out,
    stiff_pad,
    slot_pad,
    pot_pad,
    turn,
    mass_cols,
    one_hot,
    prod_own_hi,
    prod_own_lo,
    prod_ghost_hi,
    prod_ghost_lo,
    own_hi,
    own_lo,
    ghost_hi,
    ghost_lo,
    pick,
    place,
    band_out,
    band_in,
    value,
    before,
    pre,
    acc,
    ghost_out,
    ghost_in,
    back_out,
    back_in,
    band_send,
    band_recv,
    ghost_send,
    ghost_recv,
    back_send,
    back_recv,
):
    me = lax.axis_index("mesh")
    band = lax.axis_index("band")
    core = lax.rem(me, 2)
    near = (me + 1 - 2 * core, band)
    far = (lax.rem(me + parts - 1 + 2 * core, parts), band)
    other = (me, 1 - band)

    barrier = pltpu.get_barrier_semaphore()
    for device in (other, far, near):
        pl.semaphore_signal(barrier, inc=1, device_id=device, device_id_type=MESH)

    def band_copy(j):
        return pltpu.make_async_remote_copy(
            src_ref=band_out.at[j],
            dst_ref=band_in.at[j],
            send_sem=band_send.at[j],
            recv_sem=band_recv.at[j],
            device_id=other,
            device_id_type=MESH,
        )

    def chain_copies(src, dst, send, recv, k, j):
        copies = []
        for edge, device, row in ((0, far, core * GHOST), (1, near, (1 - core) * GHOST)):
            row = pl.multiple_of(row, 8)
            there = pl.multiple_of(GHOST - row, 8)
            copies.append(
                pltpu.make_async_remote_copy(
                    src_ref=src.at[k, j, pl.ds(row, GHOST)],
                    dst_ref=dst.at[k, j, pl.ds(there, GHOST)],
                    send_sem=send.at[k, j, edge],
                    recv_sem=recv.at[k, j, edge],
                    device_id=device,
                    device_id_type=MESH,
                )
            )
        return copies

    def ghost_copies(k, j):
        return chain_copies(ghost_out, ghost_in, ghost_send, ghost_recv, k, j)

    def back_copies(k, j):
        return chain_copies(back_out, back_in, back_send, back_recv, k, j)

    x_hi, x_lo = split(states[...])

    def rotated_chunk(which, j):
        at = pl.multiple_of(which * BANDW + j * W, W)
        c_hi, c_lo = split(coefficients[:, pl.ds(at, W)])
        return fold(dot(x_hi, jnp.concatenate([c_hi, c_lo], axis=1))) + dot(x_lo, c_hi)

    for j in range(2):
        band_out[j] = rotated_chunk(1 - band, j)
        if j == 0:
            pl.semaphore_wait(barrier, 3)
        band_copy(j).start()
    for j in range(2):
        value[j] = rotated_chunk(band, j)

    turn[...] = jnp.zeros_like(turn)
    turn[:, :OWN] = jnp.broadcast_to(mass[...].reshape(1, OWN), (W, OWN))
    mass_cols[...] = turn[...].T[:OWN]

    rows = jnp.concatenate([shared[0, 0:1, :], shared[0, 1:2, :]], axis=1)
    place[...] = jnp.where(
        lax.broadcasted_iota(jnp.int32, (OWN, 2 * GHOST), 0) == rows, 1.0, 0.0
    ).astype(BF16)
    turn[:, : 2 * GHOST] = jnp.broadcast_to(rows.astype(F32), (W, 2 * GHOST))
    columns = turn[:, :512].T[: 2 * GHOST].astype(jnp.int32)
    for at in range(0, OWN, W):
        width = min(W, OWN - at)
        pick[:, at : at + width] = jnp.where(
            lax.broadcasted_iota(jnp.int32, (2 * GHOST, width), 1) + at == columns[:, :width],
            1.0,
            0.0,
        ).astype(BF16)

    stiff_pad[...] = jnp.zeros_like(stiff_pad)
    stiff_pad[:NPE, :NPE] = stiffness[...]
    slot_pad[...] = jnp.full(slot_pad.shape, -1, jnp.int32)
    drawn = slots[...]
    absent = ((me == 0) & (drawn >= OWN) & (drawn < OWN + GHOST)) | (
        (me == parts - 1) & (drawn >= OWN + GHOST)
    )
    slot_pad[:CELLS, :NPE] = jnp.where(absent, -1, drawn)
    pot_pad[...] = jnp.zeros_like(pot_pad)
    pot_pad[:CELLS, :NPE] = potential[...]

    @pl.loop(0, CELLS)
    def _(c):
        at = pl.multiple_of(c * PAD, PAD)
        row = slot_pad[pl.ds(c, 1), :]
        hot = jnp.where(
            lax.broadcasted_iota(jnp.int32, (NODES, PAD), 0) == row, 1.0, 0.0
        ).astype(BF16)
        one_hot[:, pl.ds(at, PAD)] = hot
        diagonal = lax.broadcasted_iota(jnp.int32, (PAD, PAD), 0) == lax.broadcasted_iota(
            jnp.int32, (PAD, PAD), 1
        )
        cell = scale[c] * stiff_pad[...] + jnp.where(diagonal, pot_pad[pl.ds(c, 1), :], 0.0)
        stacked = jnp.concatenate(split(cell), axis=0)
        for part, high, low in (
            (hot[:OWN], prod_own_hi, prod_own_lo),
            (hot[OWN:], prod_ghost_hi, prod_ghost_lo),
        ):
            both = dot_nt(stacked, part)
            high[pl.ds(at, PAD), :], low[pl.ds(at, PAD), :] = split(both[:PAD] + both[PAD:])

    def block(rows, cols, high, low):
        left = one_hot[rows, :]
        return dot(left, high[:, cols]) + dot(left, low[:, cols])

    def own_block(at):
        end = min(at + 256, OWN)
        whole = block(slice(at, NODES), slice(at, end), prod_own_hi, prod_own_lo)
        own_hi[at:, at:end], own_lo[at:, at:end] = split(whole)
        if end < OWN:
            flipped = whole[end - at : OWN - at].T
            own_hi[at:end, end:], own_lo[at:end, end:] = split(flipped)
        ghost_hi[at:end], ghost_lo[at:end] = split(whole[OWN - at :].T)

    def ghost_block():
        for at in (0, 256):
            cols = slice(at, min(at + 256, 2 * GHOST))
            square = block(slice(OWN, NODES), cols, prod_ghost_hi, prod_ghost_lo)
            ghost_hi[OWN:, cols], ghost_lo[OWN:, cols] = split(square)

    def scatter_own(k, j):
        packed = pair(mass_cols[...] * value[j])
        ghost_out[k, j] = fold(dot(pick[...], packed))
        for copy in ghost_copies(k, j):
            copy.start()

    def own_product(j):
        pre[j] = apply_pair(own_hi[...], own_lo[...], pair(mass_cols[...] * value[j]))

    def begin(j):
        band_copy(j).wait_recv()
        value[j] = value[j] + band_in[j]
        before[j] = jnp.zeros((OWN, W), F32)
        scatter_own(0, j)

    def ghost_step(k, j):
        for copy in ghost_copies(k, j):
            copy.wait_recv()
        packed = pair(ghost_in[k, j])
        back_out[k, j] = pre[j, OWN:] + apply_pair(ghost_hi[OWN:], ghost_lo[OWN:], packed)
        for copy in back_copies(k, j):
            copy.start()
        acc[j] = pre[j, :OWN] + apply_pair(ghost_hi[:OWN], ghost_lo[:OWN], packed)

    def back_step(k, j, front, past):
        for copy in back_copies(k, j):
            copy.wait_recv()
        u = mass_cols[...] * (acc[j] + fold(dot(place[...], pair(back_in[k, j]))))
        now = value[j]
        return (u - centre * now) * front - past * before[j], now

    def finish(j):
        for copy in back_copies(last, j):
            copy.wait_recv()
        u = mass_cols[...] * (acc[j] + fold(dot(place[...], pair(back_in[last, j]))))
        front, past = COEFS[last]
        out[:, j * W : (j + 1) * W] = (u - centre * value[j]) - (past / front) * before[j]

    def advance(k, j):
        front = jnp.where(k == 0, COEFS[0][0], COEFS[1][0])
        past = jnp.where(k == 0, COEFS[0][1], COEFS[1][1])
        following, now = back_step(k, j, front, past)
        before[j] = now
        value[j] = following
        scatter_own(k + 1, j)
        own_product(j)

    own_block(0)
    ghost_block()
    begin(0)
    own_block(256)
    own_block(512)
    own_block(768)
    own_product(0)
    ghost_step(0, 0)
    begin(1)
    own_product(1)

    @pl.loop(0, DEGREE - 1)
    def _(k):
        advance(k, 0)
        ghost_step(k, 1)
        ghost_step(k + 1, 0)
        advance(k, 1)

    last = DEGREE - 1
    finish(0)
    ghost_step(last, 1)
    finish(1)

    for j in range(2):
        band_copy(j).wait_send()

    @pl.loop(0, DEGREE)
    def _(k):
        for j in range(2):
            for copy in ghost_copies(k, j) + back_copies(k, j):
                copy.wait_send()


def solution(mesh):
    parts = mesh.shape["mesh"]
    vmem = pl.BlockSpec(memory_space=pltpu.VMEM)
    smem = pl.BlockSpec(memory_space=pltpu.SMEM)
    dma = pltpu.SemaphoreType.DMA

    def body(states, mass, stiffness, scale, potential, slots, shared, coefficients):
        def run(*refs):
            kernel(parts, *refs)

        filtered = pl.pallas_call(
            run,
            out_shape=jax.ShapeDtypeStruct((OWN, BANDW), F32),
            in_specs=[vmem, vmem, vmem, smem, vmem, vmem, vmem, vmem],
            out_specs=vmem,
            scratch_shapes=[
                pltpu.VMEM((PAD, PAD), F32),
                pltpu.VMEM((8, PAD), jnp.int32),
                pltpu.VMEM((8, PAD), F32),
                pltpu.VMEM((W, 896), F32),
                pltpu.VMEM((OWN, W), F32),
                pltpu.VMEM((NODES, CELLS * PAD), BF16),
                pltpu.VMEM((CELLS * PAD, OWN), BF16),
                pltpu.VMEM((CELLS * PAD, OWN), BF16),
                pltpu.VMEM((CELLS * PAD, 2 * GHOST), BF16),
                pltpu.VMEM((CELLS * PAD, 2 * GHOST), BF16),
                pltpu.VMEM((NODES, OWN), BF16),
                pltpu.VMEM((NODES, OWN), BF16),
                pltpu.VMEM((NODES, 2 * GHOST), BF16),
                pltpu.VMEM((NODES, 2 * GHOST), BF16),
                pltpu.VMEM((2 * GHOST, OWN), BF16),
                pltpu.VMEM((OWN, 2 * GHOST), BF16),
                pltpu.VMEM((2, OWN, W), F32),
                pltpu.VMEM((2, OWN, W), F32),
                pltpu.VMEM((2, OWN, W), F32),
                pltpu.VMEM((2, OWN, W), F32),
                pltpu.VMEM((2, NODES, W), F32),
                pltpu.VMEM((2, OWN, W), F32),
                pltpu.VMEM((DEGREE, 2, 2 * GHOST, W), F32),
                pltpu.VMEM((DEGREE, 2, 2 * GHOST, W), F32),
                pltpu.VMEM((DEGREE, 2, 2 * GHOST, W), F32),
                pltpu.VMEM((DEGREE, 2, 2 * GHOST, W), F32),
                dma((2,)),
                dma((2,)),
                dma((DEGREE, 2, 2)),
                dma((DEGREE, 2, 2)),
                dma((DEGREE, 2, 2)),
                dma((DEGREE, 2, 2)),
            ],
            compiler_params=pltpu.CompilerParams(
                collective_id=0, has_side_effects=True, vmem_limit_bytes=56 * 2**20
            ),
        )(
            states,
            mass,
            stiffness,
            scale,
            potential,
            slots,
            shared,
            coefficients,
        )
        return filtered * COEFS[-1][0]

    return jax.shard_map(
        body,
        mesh=mesh,
        in_specs=(
            P("mesh", "band"),
            P("mesh"),
            P(),
            P("mesh"),
            P("mesh", None),
            P("mesh", None),
            P("mesh", None, None),
            P("band", None),
        ),
        out_specs=P("mesh", "band"),
        check_vma=False,
    )
```

```python
import jax
import jax.numpy as jnp
from jax import lax
from jax.experimental import pallas as pl
from jax.experimental.pallas import tpu as pltpu
from jax.sharding import PartitionSpec as P

MESH = pl.DeviceIdType.MESH
F32, BF16 = jnp.float32, jnp.bfloat16

DEGREE = 3
OWN = 864
GHOST = 216
EDGE = 224
BOTH = 2 * EDGE
ROWS = OWN + BOTH
NPE = 343
PAD = 384
CELLS = 4
W = 128
BANDW = 256
FAR, NEAR = 0, 1

low_end = -3.0
low_bound = 2.0
high_bound = 14.0

half_span = (high_bound - low_bound) / 2.0
centre = (high_bound + low_bound) / 2.0
sigma_first = half_span / (low_end - centre)
gamma_term = 2.0 / sigma_first


def chebyshev():
    rows = [(sigma_first / half_span, 0.0)]
    now = sigma_first
    for _ in range(DEGREE - 1):
        later = 1.0 / (gamma_term - now)
        rows.append((2.0 * later / half_span, now * later))
        now = later
    return rows


COEFS = chebyshev()


def dot(a, b):
    return jnp.dot(a, b, preferred_element_type=F32)


def dot_nt(a, b):
    return lax.dot_general(a, b, (((1,), (1,)), ((), ())), preferred_element_type=F32)


def split(x):
    high = x.astype(BF16)
    return high, (x - high.astype(F32)).astype(BF16)


def pair(x):
    return jnp.concatenate(split(x), axis=1)


def fold(y):
    return y[:, :W] + y[:, W:]


def apply_pair(high, low, packed):
    return fold(dot(high, packed)) + dot(low, packed[:, :W])


def iota(shape, dim):
    return lax.broadcasted_iota(jnp.int32, shape, dim)


def hot(mask):
    return jnp.where(mask, 1.0, 0.0).astype(BF16)


def kernel(
    parts,
    states,
    mass,
    stiffness,
    scale,
    potential,
    slots,
    shared,
    coefficients,
    out,
    stiff_pad,
    slot_pad,
    pot_pad,
    list_pad,
    turn,
    mass_sq,
    mass_inv,
    far_sq,
    one_hot,
    prod_own_hi,
    prod_own_lo,
    prod_edge_hi,
    prod_edge_lo,
    own_hi,
    own_lo,
    edge_hi,
    edge_lo,
    pick,
    place,
    same,
    info_out,
    info_in,
    band_out,
    band_in,
    now,
    before,
    pre,
    acc,
    stack,
    echo,
    ghost_out,
    ghost_in,
    back_out,
    back_in,
    info_sems,
    band_send,
    band_recv,
    ghost_send,
    ghost_recv,
    back_send,
    back_recv,
):
    me = lax.axis_index("mesh")
    band = lax.axis_index("band")
    core = lax.rem(me, 2)
    near = (me + 1 - 2 * core, band)
    far = (lax.rem(me + parts - 1 + 2 * core, parts), band)
    other = (me, 1 - band)

    barrier = pltpu.get_barrier_semaphore()
    for device in (other, far, near):
        pl.semaphore_signal(barrier, inc=1, device_id=device, device_id_type=MESH)

    def band_copy(j):
        return pltpu.make_async_remote_copy(
            src_ref=band_out.at[j],
            dst_ref=band_in.at[j],
            send_sem=band_send.at[j],
            recv_sem=band_recv.at[j],
            device_id=other,
            device_id_type=MESH,
        )

    def chain_copy(src, dst, send, recv, k, j, edge):
        return pltpu.make_async_remote_copy(
            src_ref=src.at[k, j, pl.ds(edge * EDGE, GHOST)],
            dst_ref=dst.at[k, j, edge, pl.ds(0, GHOST)],
            send_sem=send.at[k, j, edge],
            recv_sem=recv.at[k, j, edge],
            device_id=far if edge == FAR else near,
            device_id_type=MESH,
        )

    def ghost_copy(k, j, edge):
        return chain_copy(ghost_out, ghost_in, ghost_send, ghost_recv, k, j, edge)

    def back_copy(k, j, edge):
        return chain_copy(back_out, back_in, back_send, back_recv, k, j, edge)

    info_copy = pltpu.make_async_remote_copy(
        src_ref=info_out,
        dst_ref=info_in,
        send_sem=info_sems.at[0],
        recv_sem=info_sems.at[1],
        device_id=far,
        device_id_type=MESH,
    )

    x_hi, x_lo = split(states[...])

    def rotated_chunk(which, j):
        at = pl.multiple_of(which * BANDW + j * W, W)
        c_hi, c_lo = split(coefficients[:, pl.ds(at, W)])
        return fold(dot(x_hi, jnp.concatenate([c_hi, c_lo], axis=1))) + dot(x_lo, c_hi)

    for j in range(2):
        band_out[j] = rotated_chunk(1 - band, j)
        if j == 0:
            pl.semaphore_wait(barrier, 3)
        band_copy(j).start()
    for j in range(2):
        now[j] = rotated_chunk(band, j)

    list_pad[...] = jnp.full(list_pad.shape, -1, jnp.int32)
    first, second = shared[0, 0:1, :], shared[0, 1:2, :]
    list_pad[0:1, :GHOST] = jnp.where(core == 0, first, second)
    list_pad[1:2, :GHOST] = jnp.where(core == 0, second, first)
    for edge in (FAR, NEAR):
        row = list_pad[edge : edge + 1, :]
        place[edge] = hot(iota((OWN, EDGE), 0) == row[:, :EDGE])
        turn[:, :256] = jnp.broadcast_to(row.astype(F32), (W, 256))
        column = turn[:, :256].T[:EDGE]
        if edge == FAR:
            info_out[0] = column
        column = column.astype(jnp.int32)
        for at in range(0, OWN, W):
            width = min(W, OWN - at)
            pick[edge * EDGE : (edge + 1) * EDGE, at : at + width] = hot(
                iota((EDGE, width), 1) + at == column[:, :width]
            )

    turn[...] = jnp.zeros_like(turn)
    turn[:, :OWN] = jnp.broadcast_to(mass[...].reshape(1, OWN), (W, OWN))
    columns = turn[...].T[:OWN]
    mass_sq[...] = columns * columns
    mass_inv[...] = 1.0 / columns
    far_sq[...] = fold(dot(pick[:EDGE], pair(mass_sq[...])))
    info_out[1] = far_sq[...]
    info_copy.start()
    for j in range(2):
        now[j] = now[j] * columns

    edge_hi[...] = jnp.zeros_like(edge_hi)
    edge_lo[...] = jnp.zeros_like(edge_lo)
    stack[...] = jnp.zeros_like(stack)
    back_in[:, :, :, GHOST:] = jnp.zeros((DEGREE, 2, 2, EDGE - GHOST, W), F32)
    ghost_in[:, :, :, GHOST:] = jnp.zeros((DEGREE, 2, 2, EDGE - GHOST, W), F32)
    stiff_pad[...] = jnp.zeros_like(stiff_pad)
    stiff_pad[:NPE, :NPE] = stiffness[...]
    slot_pad[...] = jnp.full(slot_pad.shape, -1, jnp.int32)
    drawn = slots[...]
    is_low = (drawn >= OWN) & (drawn < OWN + GHOST)
    is_high = drawn >= OWN + GHOST
    absent = ((me == 0) & is_low) | ((me == parts - 1) & is_high)
    low_at = jnp.where(core == 0, drawn, drawn + EDGE)
    high_at = jnp.where(core == 0, drawn + (EDGE - GHOST), drawn - GHOST)
    placed = jnp.where(is_low, low_at, jnp.where(is_high, high_at, drawn))
    slot_pad[:CELLS, :NPE] = jnp.where(absent, -1, placed)
    pot_pad[...] = jnp.zeros_like(pot_pad)
    pot_pad[:CELLS, :NPE] = potential[...]

    @pl.loop(0, CELLS)
    def _(c):
        at = pl.multiple_of(c * PAD, PAD)
        row = slot_pad[pl.ds(c, 1), :]
        nodes = hot(iota((ROWS, PAD), 0) == row)
        one_hot[:, pl.ds(at, PAD)] = nodes
        diagonal = iota((PAD, PAD), 0) == iota((PAD, PAD), 1)
        cell = scale[c] * stiff_pad[...] + jnp.where(diagonal, pot_pad[pl.ds(c, 1), :], 0.0)
        stacked = jnp.concatenate(split(cell), axis=0)
        for start, size, high, low, lane in (
            (0, OWN, prod_own_hi, prod_own_lo, 0),
            (OWN, EDGE, prod_edge_hi, prod_edge_lo, 0),
            (OWN + EDGE, EDGE, prod_edge_hi, prod_edge_lo, 256),
        ):
            both = dot_nt(stacked, nodes[start : start + size])
            cols = slice(lane, lane + size)
            high[pl.ds(at, PAD), cols], low[pl.ds(at, PAD), cols] = split(both[:PAD] + both[PAD:])

    def block(rows, cols, high, low):
        left = one_hot[rows, :]
        return dot(left, high[:, cols]) + dot(left, low[:, cols])

    def own_block(at):
        end = min(at + 256, OWN)
        whole = block(slice(at, ROWS), slice(at, end), prod_own_hi, prod_own_lo)
        own_hi[at:, at:end], own_lo[at:, at:end] = split(whole)
        if end < OWN:
            flipped = whole[end - at : OWN - at].T
            own_hi[at:end, end:], own_lo[at:end, end:] = split(flipped)
        for edge in (FAR, NEAR):
            row = OWN - at + edge * EDGE
            cols = slice((edge + 1) * 256, (edge + 1) * 256 + EDGE)
            edge_hi[at:end, cols], edge_lo[at:end, cols] = split(whole[row : row + EDGE].T)

    def edge_block():
        for edge in (FAR, NEAR):
            cols = slice(edge * 256, edge * 256 + EDGE)
            to = slice((edge + 1) * 256, (edge + 1) * 256 + EDGE)
            square = block(slice(OWN, ROWS), cols, prod_edge_hi, prod_edge_lo)
            edge_hi[OWN:, to], edge_lo[OWN:, to] = split(square)

    def far_columns():
        edge_hi[:, :EDGE] = dot(own_hi[...], place[FAR]).astype(BF16)
        edge_lo[:, :EDGE] = dot(own_lo[...], place[FAR]).astype(BF16)

    def begin(j):
        band_copy(j).wait_recv()
        now[j] = now[j] + mass_cols() * band_in[j]
        ghost_out[0, j] = fold(dot(pick[...], pair(now[j])))
        ghost_copy(0, j, FAR).start()
        ghost_copy(0, j, NEAR).start()

    def mass_cols():
        return mass_sq[...] * mass_inv[...]

    def own_product(j):
        pre[j] = apply_pair(own_hi[...], own_lo[...], pair(now[j]))

    def contribute(k, j):
        for edge in (NEAR, FAR):
            ghost_copy(k, j, edge).wait_recv()
        far_ghost = ghost_in[k, j, FAR]
        if k > 0:
            far_ghost = far_ghost + COEFS[k - 1][0] * echo[j]
        stack[j, 256 : 256 + EDGE] = far_ghost
        stack[j, 512 : 512 + EDGE] = ghost_in[k, j, NEAR]
        start = 0 if k > 0 else 256
        packed = pair(stack[j, start:])
        sent = pre[j, OWN:] + apply_pair(edge_hi[OWN:, start:], edge_lo[OWN:, start:], packed)
        back_out[k, j] = sent
        back_copy(k, j, NEAR).start()
        back_copy(k, j, FAR).start()
        acc[j] = pre[j, :OWN] + apply_pair(edge_hi[:OWN, start:], edge_lo[:OWN, start:], packed)
        if k < DEGREE - 1:
            echo[j] = info_in[1] * fold(dot(same[...], pair(sent[:EDGE])))

    def settle_chip(k, j):
        back_copy(k, j, NEAR).wait_recv()
        front, past = COEFS[k]
        raw = acc[j] + fold(dot(place[NEAR], pair(back_in[k, j, NEAR])))
        current = now[j]
        following = front * (mass_sq[...] * raw - centre * current)
        if k > 0:
            following = following - past * before[j]
        packed = pair(following)
        ghost_out[k + 1, j, :EDGE] = fold(dot(pick[:EDGE], packed))
        ghost_copy(k + 1, j, FAR).start()
        before[j] = current
        now[j] = following
        pre[j] = apply_pair(own_hi[...], own_lo[...], packed)

    def settle_far(k, j):
        back_copy(k, j, FAR).wait_recv()
        change = COEFS[k][0] * far_sq[...] * back_in[k, j, FAR]
        stack[j, :EDGE] = change
        following = now[j] + fold(dot(place[FAR], pair(change)))
        ghost_out[k + 1, j, EDGE:] = fold(dot(pick[EDGE:], pair(following)))
        ghost_copy(k + 1, j, NEAR).start()
        now[j] = following

    def finish(j):
        last = DEGREE - 1
        back_copy(last, j, NEAR).wait_recv()
        raw = acc[j] + fold(dot(place[NEAR], pair(back_in[last, j, NEAR])))
        front, past = COEFS[last]
        rest = centre * now[j] + (past / front) * before[j]
        back_copy(last, j, FAR).wait_recv()
        raw = raw + fold(dot(place[FAR], pair(back_in[last, j, FAR])))
        out[:, j * W : (j + 1) * W] = mass_inv[...] * (mass_sq[...] * raw - rest)

    own_block(0)
    edge_block()
    info_copy.wait_recv()
    theirs = info_in[0]
    turn[:, :256] = jnp.concatenate([theirs, jnp.zeros((256 - EDGE, W), F32)], axis=0).T
    same[...] = hot(
        jnp.concatenate([theirs, theirs[:, : EDGE - W]], axis=1) == turn[0:1, :EDGE]
    )
    begin(0)
    own_block(256)
    own_block(512)
    own_block(768)
    far_columns()
    own_product(0)
    contribute(0, 0)
    settle_chip(0, 0)
    begin(1)
    own_product(1)
    settle_far(0, 0)
    contribute(0, 1)
    settle_chip(0, 1)
    contribute(1, 0)
    settle_chip(1, 0)
    settle_far(0, 1)
    contribute(1, 1)
    settle_chip(1, 1)
    settle_far(1, 0)
    contribute(2, 0)
    settle_far(1, 1)
    contribute(2, 1)
    finish(0)
    finish(1)

    info_copy.wait_send()
    for j in range(2):
        band_copy(j).wait_send()

    @pl.loop(0, DEGREE)
    def _(k):
        for j in range(2):
            for edge in (FAR, NEAR):
                ghost_copy(k, j, edge).wait_send()
                back_copy(k, j, edge).wait_send()


def solution(mesh):
    parts = mesh.shape["mesh"]
    vmem = pl.BlockSpec(memory_space=pltpu.VMEM)
    smem = pl.BlockSpec(memory_space=pltpu.SMEM)
    dma = pltpu.SemaphoreType.DMA

    def body(states, mass, stiffness, scale, potential, slots, shared, coefficients):
        def run(*refs):
            kernel(parts, *refs)

        filtered = pl.pallas_call(
            run,
            out_shape=jax.ShapeDtypeStruct((OWN, BANDW), F32),
            in_specs=[vmem, vmem, vmem, smem, vmem, vmem, vmem, vmem],
            out_specs=vmem,
            scratch_shapes=[
                pltpu.VMEM((PAD, PAD), F32),
                pltpu.VMEM((8, PAD), jnp.int32),
                pltpu.VMEM((8, PAD), F32),
                pltpu.VMEM((8, 256), jnp.int32),
                pltpu.VMEM((W, 896), F32),
                pltpu.VMEM((OWN, W), F32),
                pltpu.VMEM((OWN, W), F32),
                pltpu.VMEM((EDGE, W), F32),
                pltpu.VMEM((ROWS, CELLS * PAD), BF16),
                pltpu.VMEM((CELLS * PAD, OWN), BF16),
                pltpu.VMEM((CELLS * PAD, OWN), BF16),
                pltpu.VMEM((CELLS * PAD, 512), BF16),
                pltpu.VMEM((CELLS * PAD, 512), BF16),
                pltpu.VMEM((ROWS, OWN), BF16),
                pltpu.VMEM((ROWS, OWN), BF16),
                pltpu.VMEM((ROWS, 768), BF16),
                pltpu.VMEM((ROWS, 768), BF16),
                pltpu.VMEM((BOTH, OWN), BF16),
                pltpu.VMEM((2, OWN, EDGE), BF16),
                pltpu.VMEM((EDGE, EDGE), BF16),
                pltpu.VMEM((2, EDGE, W), F32),
                pltpu.VMEM((2, EDGE, W), F32),
                pltpu.VMEM((2, OWN, W), F32),
                pltpu.VMEM((2, OWN, W), F32),
                pltpu.VMEM((2, OWN, W), F32),
                pltpu.VMEM((2, OWN, W), F32),
                pltpu.VMEM((2, ROWS, W), F32),
                pltpu.VMEM((2, OWN, W), F32),
                pltpu.VMEM((2, 768, W), F32),
                pltpu.VMEM((2, EDGE, W), F32),
                pltpu.VMEM((DEGREE, 2, BOTH, W), F32),
                pltpu.VMEM((DEGREE, 2, 2, EDGE, W), F32),
                pltpu.VMEM((DEGREE, 2, BOTH, W), F32),
                pltpu.VMEM((DEGREE, 2, 2, EDGE, W), F32),
                dma((2,)),
                dma((2,)),
                dma((2,)),
                dma((DEGREE, 2, 2)),
                dma((DEGREE, 2, 2)),
                dma((DEGREE, 2, 2)),
                dma((DEGREE, 2, 2)),
            ],
            compiler_params=pltpu.CompilerParams(
                collective_id=0, has_side_effects=True, vmem_limit_bytes=56 * 2**20
            ),
        )(states, mass, stiffness, scale, potential, slots, shared, coefficients)
        return filtered * COEFS[-1][0]

    return jax.shard_map(
        body,
        mesh=mesh,
        in_specs=(
            P("mesh", "band"),
            P("mesh"),
            P(),
            P("mesh"),
            P("mesh", None),
            P("mesh", None),
            P("mesh", None, None),
            P("band", None),
        ),
        out_specs=P("mesh", "band"),
        check_vma=False,
    )
```

```python
import jax
import jax.numpy as jnp
from jax import lax
from jax.experimental import pallas as pl
from jax.experimental.pallas import tpu as pltpu
from jax.sharding import PartitionSpec as P

MESH = pl.DeviceIdType.MESH
F32, BF16 = jnp.float32, jnp.bfloat16

DEGREE = 3
OWN = 864
GHOST = 216
EDGE = 224
HALF = OWN // 2
BOTH = 2 * EDGE
ROWS = OWN + BOTH
NPE = 343
PAD = 384
CELLS = 4
W = 128
BANDW = 256
FAR, NEAR = 0, 1

low_end = -3.0
low_bound = 2.0
high_bound = 14.0

half_span = (high_bound - low_bound) / 2.0
centre = (high_bound + low_bound) / 2.0
sigma_first = half_span / (low_end - centre)
gamma_term = 2.0 / sigma_first


def chebyshev():
    rows = [(sigma_first / half_span, 0.0)]
    now = sigma_first
    for _ in range(DEGREE - 1):
        later = 1.0 / (gamma_term - now)
        rows.append((2.0 * later / half_span, now * later))
        now = later
    return rows


COEFS = chebyshev()


def dot(a, b):
    return jnp.dot(a, b, preferred_element_type=F32)


def dot_nt(a, b):
    return lax.dot_general(a, b, (((1,), (1,)), ((), ())), preferred_element_type=F32)


def split(x):
    high = x.astype(BF16)
    return high, (x - high.astype(F32)).astype(BF16)


def pair(x):
    return jnp.concatenate(split(x), axis=1)


def fold(y):
    return y[:, :W] + y[:, W:]


def apply_pair(high, low, packed):
    return fold(dot(high, packed)) + dot(low, packed[:, :W])


def iota(shape, dim):
    return lax.broadcasted_iota(jnp.int32, shape, dim)


def hot(mask):
    return jnp.where(mask, 1.0, 0.0).astype(BF16)


def kernel(
    parts,
    states,
    mass,
    stiffness,
    scale,
    potential,
    slots,
    shared,
    coefficients,
    out,
    stiff_pad,
    slot_pad,
    pot_pad,
    list_pad,
    turn,
    mass_sq,
    mass_inv,
    far_sq,
    one_hot,
    prod_own_hi,
    prod_own_lo,
    prod_edge_hi,
    prod_edge_lo,
    own_hi,
    own_lo,
    edge_hi,
    edge_lo,
    pick,
    place,
    same,
    order,
    back_order,
    info_out,
    info_in,
    band_out,
    band_in,
    now,
    before,
    pre,
    acc,
    stack,
    stack_pair,
    own_pair,
    echo,
    ghost_out,
    ghost_in,
    back_out,
    back_in,
    info_sems,
    band_send,
    band_recv,
    ghost_send,
    ghost_recv,
    back_send,
    back_recv,
):
    me = lax.axis_index("mesh")
    band = lax.axis_index("band")
    core = lax.rem(me, 2)
    near = (me + 1 - 2 * core, band)
    far = (lax.rem(me + parts - 1 + 2 * core, parts), band)
    other = (me, 1 - band)

    barrier = pltpu.get_barrier_semaphore()
    for device in (other, far, near):
        pl.semaphore_signal(barrier, inc=1, device_id=device, device_id_type=MESH)

    def band_copy(part):
        piece = (0,) if part == 0 else (1, pl.ds((part - 1) * HALF, HALF))
        return pltpu.make_async_remote_copy(
            src_ref=band_out.at[piece],
            dst_ref=band_in.at[piece],
            send_sem=band_send.at[part],
            recv_sem=band_recv.at[part],
            device_id=other,
            device_id_type=MESH,
        )

    def chain_copy(src, dst, send, recv, k, j, edge):
        return pltpu.make_async_remote_copy(
            src_ref=src.at[k, j, pl.ds(edge * EDGE, GHOST)],
            dst_ref=dst.at[k, j, edge, pl.ds(0, GHOST)],
            send_sem=send.at[k, j, edge],
            recv_sem=recv.at[k, j, edge],
            device_id=far if edge == FAR else near,
            device_id_type=MESH,
        )

    def ghost_copy(k, j, edge):
        return chain_copy(ghost_out, ghost_in, ghost_send, ghost_recv, k, j, edge)

    def back_copy(k, j, edge):
        return chain_copy(back_out, back_in, back_send, back_recv, k, j, edge)

    info_copy = pltpu.make_async_remote_copy(
        src_ref=info_out,
        dst_ref=info_in,
        send_sem=info_sems.at[0],
        recv_sem=info_sems.at[1],
        device_id=far,
        device_id_type=MESH,
    )

    x_hi, x_lo = split(states[...])

    def rotated_chunk(which, j):
        at = pl.multiple_of(which * BANDW + j * W, W)
        c_hi, c_lo = split(coefficients[:, pl.ds(at, W)])
        return fold(dot(x_hi, jnp.concatenate([c_hi, c_lo], axis=1))) + dot(x_lo, c_hi)

    band_out[0] = rotated_chunk(1 - band, 0)
    pl.semaphore_wait(barrier, 3)
    band_copy(0).start()

    list_pad[...] = jnp.full(list_pad.shape, -1, jnp.int32)
    first, second = shared[0, 0:1, :], shared[0, 1:2, :]
    list_pad[0:1, :GHOST] = jnp.where(core == 0, first, second)
    list_pad[1:2, :GHOST] = jnp.where(core == 0, second, first)

    def along_rows(row, length):
        turn[:, :length] = jnp.broadcast_to(row.astype(F32), (W, length))

    for edge in (FAR, NEAR):
        row = list_pad[edge : edge + 1, :]
        place[edge] = hot(iota((OWN, EDGE), 0) == row[:, :EDGE])
        along_rows(row, 256)
        column = turn[:, :256].T[:EDGE]
        if edge == FAR:
            info_out[0] = column
        column = column.astype(jnp.int32)
        for at in range(0, OWN, W):
            width = min(W, OWN - at)
            pick[edge * EDGE : (edge + 1) * EDGE, at : at + width] = hot(
                iota((EDGE, width), 1) + at == column[:, :width]
            )

    counts = dot(jnp.ones((16, BOTH), BF16), pick[...])
    is_shared = counts > 0.5
    ahead = dot(hot(is_shared), hot(iota((OWN, OWN), 0) < iota((OWN, OWN), 1)))[0:1]
    is_shared = is_shared[0:1]
    total = jnp.sum(jnp.where(is_shared, 1.0, 0.0), axis=1, keepdims=True)
    here = lax.broadcasted_iota(jnp.int32, (1, OWN), 1).astype(F32)
    rank = jnp.where(is_shared, ahead, total + here - ahead)
    order[...] = hot(iota((OWN, OWN), 0) == rank.astype(jnp.int32))
    band_out[1] = fold(dot(order[...], pair(rotated_chunk(1 - band, 1))))
    for part in (1, 2):
        band_copy(part).start()
    turn[:, OWN:] = jnp.zeros((W, 896 - OWN), F32)
    along_rows(rank, OWN)
    column = turn[...].T[:OWN].astype(jnp.int32)
    for half in range(2):
        for at in range(0, HALF, W):
            width = min(W, HALF - at)
            back_order[half, :, at : at + width] = hot(
                iota((OWN, width), 1) + (half * HALF + at) == column[:, :width]
            )
    for j in range(2):
        now[j] = rotated_chunk(band, j)

    turn[...] = jnp.zeros_like(turn)
    turn[:, :OWN] = jnp.broadcast_to(mass[...].reshape(1, OWN), (W, OWN))
    columns = turn[...].T[:OWN]
    mass_sq[...] = columns * columns
    mass_inv[...] = 1.0 / columns
    far_sq[...] = fold(dot(pick[:EDGE], pair(mass_sq[...])))
    info_out[1] = far_sq[...]
    info_copy.start()
    for j in range(2):
        now[j] = now[j] * columns

    edge_hi[...] = jnp.zeros_like(edge_hi)
    edge_lo[...] = jnp.zeros_like(edge_lo)
    stack[...] = jnp.zeros_like(stack)
    back_in[:, :, :, GHOST:] = jnp.zeros((DEGREE, 2, 2, EDGE - GHOST, W), F32)
    ghost_in[:, :, :, GHOST:] = jnp.zeros((DEGREE, 2, 2, EDGE - GHOST, W), F32)
    stiff_pad[...] = jnp.zeros_like(stiff_pad)
    stiff_pad[:NPE, :NPE] = stiffness[...]
    slot_pad[...] = jnp.full(slot_pad.shape, -1, jnp.int32)
    drawn = slots[...]
    is_low = (drawn >= OWN) & (drawn < OWN + GHOST)
    is_high = drawn >= OWN + GHOST
    absent = ((me == 0) & is_low) | ((me == parts - 1) & is_high)
    low_at = jnp.where(core == 0, drawn, drawn + EDGE)
    high_at = jnp.where(core == 0, drawn + (EDGE - GHOST), drawn - GHOST)
    placed = jnp.where(is_low, low_at, jnp.where(is_high, high_at, drawn))
    slot_pad[:CELLS, :NPE] = jnp.where(absent, -1, placed)
    pot_pad[...] = jnp.zeros_like(pot_pad)
    pot_pad[:CELLS, :NPE] = potential[...]

    @pl.loop(0, CELLS)
    def _(c):
        at = pl.multiple_of(c * PAD, PAD)
        row = slot_pad[pl.ds(c, 1), :]
        nodes = hot(iota((ROWS, PAD), 0) == row)
        one_hot[:, pl.ds(at, PAD)] = nodes
        diagonal = iota((PAD, PAD), 0) == iota((PAD, PAD), 1)
        cell = scale[c] * stiff_pad[...] + jnp.where(diagonal, pot_pad[pl.ds(c, 1), :], 0.0)
        stacked = jnp.concatenate(split(cell), axis=0)
        for start, size, high, low, lane in (
            (0, OWN, prod_own_hi, prod_own_lo, 0),
            (OWN, EDGE, prod_edge_hi, prod_edge_lo, 0),
            (OWN + EDGE, EDGE, prod_edge_hi, prod_edge_lo, 256),
        ):
            both = dot_nt(stacked, nodes[start : start + size])
            cols = slice(lane, lane + size)
            high[pl.ds(at, PAD), cols], low[pl.ds(at, PAD), cols] = split(both[:PAD] + both[PAD:])

    def block(rows, cols, high, low):
        left = one_hot[rows, :]
        return dot(left, high[:, cols]) + dot(left, low[:, cols])

    def own_block(at):
        end = min(at + 256, OWN)
        whole = block(slice(at, OWN), slice(at, end), prod_own_hi, prod_own_lo)
        own_hi[at:OWN, at:end], own_lo[at:OWN, at:end] = split(whole)
        if end < OWN:
            own_hi[at:end, end:], own_lo[at:end, end:] = split(whole[end - at :].T)

    def edge_rows(at):
        end = min(at + 256, OWN)
        whole = block(slice(OWN, ROWS), slice(at, end), prod_own_hi, prod_own_lo)
        own_hi[OWN:, at:end], own_lo[OWN:, at:end] = split(whole)
        for edge in (FAR, NEAR):
            cols = slice((edge + 1) * 256, (edge + 1) * 256 + EDGE)
            flipped = whole[edge * EDGE : (edge + 1) * EDGE].T
            edge_hi[at:end, cols], edge_lo[at:end, cols] = split(flipped)

    def edge_block():
        for edge in (FAR, NEAR):
            cols = slice(edge * 256, edge * 256 + EDGE)
            to = slice((edge + 1) * 256, (edge + 1) * 256 + EDGE)
            square = block(slice(OWN, ROWS), cols, prod_edge_hi, prod_edge_lo)
            edge_hi[OWN:, to], edge_lo[OWN:, to] = split(square)

    def far_columns():
        edge_hi[:, :EDGE] = dot(own_hi[...], place[FAR]).astype(BF16)
        edge_lo[:, :EDGE] = dot(own_lo[...], place[FAR]).astype(BF16)

    def begin(j):
        ghost_out[0, j] = fold(dot(pick[...], pair(now[j])))
        ghost_copy(0, j, FAR).start()
        ghost_copy(0, j, NEAR).start()

    def begin_whole():
        band_copy(0).wait_recv()
        now[0] = now[0] + mass_cols() * band_in[0]
        own_pair[0] = pair(now[0])
        begin(0)

    def begin_half(half):
        band_copy(1 + half).wait_recv()
        arrived = pair(band_in[1, half * HALF : (half + 1) * HALF])
        now[1] = now[1] + mass_cols() * fold(dot(back_order[half], arrived))
        if half == 0:
            begin(1)
        else:
            own_pair[1] = pair(now[1])

    def mass_cols():
        return mass_sq[...] * mass_inv[...]

    def own_product(j):
        pre[j] = apply_pair(own_hi[...], own_lo[...], own_pair[j])

    def contribute(k, j):
        for edge in (NEAR, FAR):
            ghost_copy(k, j, edge).wait_recv()
        far_ghost = ghost_in[k, j, FAR]
        if k > 0:
            far_ghost = far_ghost + COEFS[k - 1][0] * echo[j]
        stack[j, 256 : 256 + EDGE] = far_ghost
        stack[j, 512 : 512 + EDGE] = ghost_in[k, j, NEAR]
        start = 0 if k > 0 else 256
        packed = pair(stack[j, start:])
        stack_pair[j, start:] = packed
        back_out[k, j] = pre[j, OWN:] + apply_pair(
            edge_hi[OWN:, start:], edge_lo[OWN:, start:], packed
        )
        back_copy(k, j, NEAR).start()
        back_copy(k, j, FAR).start()

    def gather_own(k, j):
        start = 0 if k > 0 else 256
        acc[j] = pre[j, :OWN] + apply_pair(
            edge_hi[:OWN, start:], edge_lo[:OWN, start:], stack_pair[j, start:]
        )
        if k < DEGREE - 1:
            echo[j] = info_in[1] * fold(dot(same[...], pair(back_out[k, j, :EDGE])))

    def settle_chip(k, j):
        back_copy(k, j, NEAR).wait_recv()
        front, past = COEFS[k]
        raw = acc[j] + fold(dot(place[NEAR], pair(back_in[k, j, NEAR])))
        current = now[j]
        following = front * (mass_sq[...] * raw - centre * current)
        if k > 0:
            following = following - past * before[j]
        packed = pair(following)
        own_pair[j] = packed
        ghost_out[k + 1, j, :EDGE] = fold(dot(pick[:EDGE], packed))
        ghost_copy(k + 1, j, FAR).start()
        before[j] = current
        now[j] = following

    def settle_far(k, j):
        back_copy(k, j, FAR).wait_recv()
        change = COEFS[k][0] * far_sq[...] * back_in[k, j, FAR]
        stack[j, :EDGE] = change
        following = now[j] + fold(dot(place[FAR], pair(change)))
        ghost_out[k + 1, j, EDGE:] = fold(dot(pick[EDGE:], pair(following)))
        ghost_copy(k + 1, j, NEAR).start()
        now[j] = following

    def finish(j):
        last = DEGREE - 1
        back_copy(last, j, NEAR).wait_recv()
        raw = acc[j] + fold(dot(place[NEAR], pair(back_in[last, j, NEAR])))
        front, past = COEFS[last]
        rest = centre * now[j] + (past / front) * before[j]
        back_copy(last, j, FAR).wait_recv()
        raw = raw + fold(dot(place[FAR], pair(back_in[last, j, FAR])))
        out[:, j * W : (j + 1) * W] = mass_inv[...] * (mass_sq[...] * raw - rest)

    own_block(0)
    own_block(256)
    own_block(512)
    own_block(768)
    begin_whole()
    for at in range(0, OWN, 256):
        edge_rows(at)
    edge_block()
    info_copy.wait_recv()
    theirs = info_in[0]
    turn[:, :256] = jnp.concatenate([theirs, jnp.zeros((256 - EDGE, W), F32)], axis=0).T
    same[...] = hot(
        jnp.concatenate([theirs, theirs[:, : EDGE - W]], axis=1) == turn[0:1, :EDGE]
    )
    own_product(0)
    begin_half(0)
    contribute(0, 0)
    gather_own(0, 0)
    settle_chip(0, 0)
    own_product(0)
    begin_half(1)
    own_product(1)
    contribute(0, 1)
    settle_far(0, 0)
    gather_own(0, 1)
    settle_chip(0, 1)
    own_product(1)
    far_columns()
    contribute(1, 0)
    settle_far(0, 1)
    gather_own(1, 0)
    settle_chip(1, 0)
    contribute(1, 1)
    gather_own(1, 1)
    settle_chip(1, 1)
    own_product(1)
    settle_far(1, 0)
    own_product(0)
    contribute(2, 0)
    settle_far(1, 1)
    contribute(2, 1)
    gather_own(2, 1)
    gather_own(2, 0)
    finish(0)
    finish(1)

    info_copy.wait_send()
    for part in range(3):
        band_copy(part).wait_send()

    @pl.loop(0, DEGREE)
    def _(k):
        for j in range(2):
            for edge in (FAR, NEAR):
                ghost_copy(k, j, edge).wait_send()
                back_copy(k, j, edge).wait_send()


def solution(mesh):
    parts = mesh.shape["mesh"]
    vmem = pl.BlockSpec(memory_space=pltpu.VMEM)
    smem = pl.BlockSpec(memory_space=pltpu.SMEM)
    dma = pltpu.SemaphoreType.DMA

    def body(states, mass, stiffness, scale, potential, slots, shared, coefficients):
        def run(*refs):
            kernel(parts, *refs)

        filtered = pl.pallas_call(
            run,
            out_shape=jax.ShapeDtypeStruct((OWN, BANDW), F32),
            in_specs=[vmem, vmem, vmem, smem, vmem, vmem, vmem, vmem],
            out_specs=vmem,
            scratch_shapes=[
                pltpu.VMEM((PAD, PAD), F32),
                pltpu.VMEM((8, PAD), jnp.int32),
                pltpu.VMEM((8, PAD), F32),
                pltpu.VMEM((8, 256), jnp.int32),
                pltpu.VMEM((W, 896), F32),
                pltpu.VMEM((OWN, W), F32),
                pltpu.VMEM((OWN, W), F32),
                pltpu.VMEM((EDGE, W), F32),
                pltpu.VMEM((ROWS, CELLS * PAD), BF16),
                pltpu.VMEM((CELLS * PAD, OWN), BF16),
                pltpu.VMEM((CELLS * PAD, OWN), BF16),
                pltpu.VMEM((CELLS * PAD, 512), BF16),
                pltpu.VMEM((CELLS * PAD, 512), BF16),
                pltpu.VMEM((ROWS, OWN), BF16),
                pltpu.VMEM((ROWS, OWN), BF16),
                pltpu.VMEM((ROWS, 768), BF16),
                pltpu.VMEM((ROWS, 768), BF16),
                pltpu.VMEM((BOTH, OWN), BF16),
                pltpu.VMEM((2, OWN, EDGE), BF16),
                pltpu.VMEM((EDGE, EDGE), BF16),
                pltpu.VMEM((OWN, OWN), BF16),
                pltpu.VMEM((2, OWN, HALF), BF16),
                pltpu.VMEM((2, EDGE, W), F32),
                pltpu.VMEM((2, EDGE, W), F32),
                pltpu.VMEM((2, OWN, W), F32),
                pltpu.VMEM((2, OWN, W), F32),
                pltpu.VMEM((2, OWN, W), F32),
                pltpu.VMEM((2, OWN, W), F32),
                pltpu.VMEM((2, ROWS, W), F32),
                pltpu.VMEM((2, OWN, W), F32),
                pltpu.VMEM((2, 768, W), F32),
                pltpu.VMEM((2, 768, 2 * W), BF16),
                pltpu.VMEM((2, OWN, 2 * W), BF16),
                pltpu.VMEM((2, EDGE, W), F32),
                pltpu.VMEM((DEGREE, 2, BOTH, W), F32),
                pltpu.VMEM((DEGREE, 2, 2, EDGE, W), F32),
                pltpu.VMEM((DEGREE, 2, BOTH, W), F32),
                pltpu.VMEM((DEGREE, 2, 2, EDGE, W), F32),
                dma((2,)),
                dma((3,)),
                dma((3,)),
                dma((DEGREE, 2, 2)),
                dma((DEGREE, 2, 2)),
                dma((DEGREE, 2, 2)),
                dma((DEGREE, 2, 2)),
            ],
            compiler_params=pltpu.CompilerParams(
                collective_id=0, has_side_effects=True, vmem_limit_bytes=46 * 2**20
            ),
        )(states, mass, stiffness, scale, potential, slots, shared, coefficients)
        return filtered * COEFS[-1][0]

    return jax.shard_map(
        body,
        mesh=mesh,
        in_specs=(
            P("mesh", "band"),
            P("mesh"),
            P(),
            P("mesh"),
            P("mesh", None),
            P("mesh", None),
            P("mesh", None, None),
            P("band", None),
        ),
        out_specs=P("mesh", "band"),
        check_vma=False,
    )
```

```python
import jax
import jax.numpy as jnp
from jax import lax
from jax.experimental import pallas as pl
from jax.experimental.pallas import tpu as pltpu
from jax.sharding import PartitionSpec as P

MESH = pl.DeviceIdType.MESH
F32, BF16 = jnp.float32, jnp.bfloat16

DEGREE = 3
OWN = 864
GHOST = 216
EDGE = 224
HALF = OWN // 2
BOTH = 2 * EDGE
ROWS = OWN + BOTH
NPE = 343
PAD = 384
CELLS = 4
W = 128
BANDW = 256
FAR, NEAR = 0, 1

low_end = -3.0
low_bound = 2.0
high_bound = 14.0

half_span = (high_bound - low_bound) / 2.0
centre = (high_bound + low_bound) / 2.0
sigma_first = half_span / (low_end - centre)
gamma_term = 2.0 / sigma_first


def chebyshev():
    rows = [(sigma_first / half_span, 0.0)]
    now = sigma_first
    for _ in range(DEGREE - 1):
        later = 1.0 / (gamma_term - now)
        rows.append((2.0 * later / half_span, now * later))
        now = later
    return rows


COEFS = chebyshev()


def dot(a, b):
    return jnp.dot(a, b, preferred_element_type=F32)


def dot_nt(a, b):
    return lax.dot_general(a, b, (((1,), (1,)), ((), ())), preferred_element_type=F32)


def split(x):
    high = x.astype(BF16)
    return high, (x - high.astype(F32)).astype(BF16)


def pair(x):
    return jnp.concatenate(split(x), axis=1)


def fold(y):
    return y[:, :W] + y[:, W:]


def apply_pair(high, low, packed):
    return fold(dot(high, packed)) + dot(low, packed[:, :W])


def iota(shape, dim):
    return lax.broadcasted_iota(jnp.int32, shape, dim)


def hot(mask):
    return jnp.where(mask, 1.0, 0.0).astype(BF16)


def kernel(
    parts,
    states_at,
    mass_at,
    stiffness_at,
    scale,
    potential_at,
    slots_at,
    shared_at,
    coefficients_at,
    out,
    states,
    coefficients,
    shared,
    mass,
    stiffness,
    potential,
    slots,
    load_sems,
    stiff_pad,
    slot_pad,
    pot_pad,
    list_pad,
    turn,
    mass_sq,
    mass_inv,
    far_sq,
    one_hot,
    prod_own_hi,
    prod_own_lo,
    prod_edge_hi,
    prod_edge_lo,
    own_hi,
    own_lo,
    edge_hi,
    edge_lo,
    pick,
    place,
    same,
    order,
    back_order,
    info_out,
    info_in,
    band_out,
    band_in,
    now,
    before,
    pre,
    acc,
    stack,
    stack_pair,
    own_pair,
    echo,
    ghost_out,
    ghost_in,
    back_out,
    back_in,
    info_sems,
    band_send,
    band_recv,
    ghost_send,
    ghost_recv,
    back_send,
    back_recv,
):
    me = lax.axis_index("mesh")
    band = lax.axis_index("band")
    loads = [
        pltpu.make_async_copy(source, target, load_sems.at[at])
        for at, (source, target) in enumerate(
            (
                (states_at, states),
                (coefficients_at, coefficients),
                (shared_at, shared),
                (mass_at, mass),
                (stiffness_at, stiffness),
                (potential_at, potential),
                (slots_at, slots),
            )
        )
    ]
    for load in loads:
        load.start()

    core = lax.rem(me, 2)
    near = (me + 1 - 2 * core, band)
    far = (lax.rem(me + parts - 1 + 2 * core, parts), band)
    other = (me, 1 - band)

    barrier = pltpu.get_barrier_semaphore()
    for device in (other, far, near):
        pl.semaphore_signal(barrier, inc=1, device_id=device, device_id_type=MESH)

    def band_copy(part):
        piece = (0,) if part == 0 else (1, pl.ds((part - 1) * HALF, HALF))
        return pltpu.make_async_remote_copy(
            src_ref=band_out.at[piece],
            dst_ref=band_in.at[piece],
            send_sem=band_send.at[part],
            recv_sem=band_recv.at[part],
            device_id=other,
            device_id_type=MESH,
        )

    def chain_copy(src, dst, send, recv, k, j, edge):
        return pltpu.make_async_remote_copy(
            src_ref=src.at[k, j, pl.ds(edge * EDGE, GHOST)],
            dst_ref=dst.at[k, j, edge, pl.ds(0, GHOST)],
            send_sem=send.at[k, j, edge],
            recv_sem=recv.at[k, j, edge],
            device_id=far if edge == FAR else near,
            device_id_type=MESH,
        )

    def ghost_copy(k, j, edge):
        return chain_copy(ghost_out, ghost_in, ghost_send, ghost_recv, k, j, edge)

    def back_copy(k, j, edge):
        return chain_copy(back_out, back_in, back_send, back_recv, k, j, edge)

    info_copy = pltpu.make_async_remote_copy(
        src_ref=info_out,
        dst_ref=info_in,
        send_sem=info_sems.at[0],
        recv_sem=info_sems.at[1],
        device_id=far,
        device_id_type=MESH,
    )

    loads[0].wait()
    loads[1].wait()
    x_hi, x_lo = split(states[...])

    def rotated_chunk(which, j):
        at = pl.multiple_of(which * BANDW + j * W, W)
        c_hi, c_lo = split(coefficients[:, pl.ds(at, W)])
        return fold(dot(x_hi, jnp.concatenate([c_hi, c_lo], axis=1))) + dot(x_lo, c_hi)

    band_out[0] = rotated_chunk(1 - band, 0)
    pl.semaphore_wait(barrier, 3)
    band_copy(0).start()

    for load in loads[2:]:
        load.wait()
    list_pad[...] = jnp.full(list_pad.shape, -1, jnp.int32)
    first, second = shared[0, 0:1, :], shared[0, 1:2, :]
    list_pad[0:1, :GHOST] = jnp.where(core == 0, first, second)
    list_pad[1:2, :GHOST] = jnp.where(core == 0, second, first)

    def along_rows(row, length):
        turn[:, :length] = jnp.broadcast_to(row.astype(F32), (W, length))

    for edge in (FAR, NEAR):
        row = list_pad[edge : edge + 1, :]
        place[edge] = hot(iota((OWN, EDGE), 0) == row[:, :EDGE])
        along_rows(row, 256)
        column = turn[:, :256].T[:EDGE]
        if edge == FAR:
            info_out[0] = column
        column = column.astype(jnp.int32)
        for at in range(0, OWN, W):
            width = min(W, OWN - at)
            pick[edge * EDGE : (edge + 1) * EDGE, at : at + width] = hot(
                iota((EDGE, width), 1) + at == column[:, :width]
            )

    counts = dot(jnp.ones((16, BOTH), BF16), pick[...])
    is_shared = counts > 0.5
    ahead = dot(hot(is_shared), hot(iota((OWN, OWN), 0) < iota((OWN, OWN), 1)))[0:1]
    is_shared = is_shared[0:1]
    total = jnp.sum(jnp.where(is_shared, 1.0, 0.0), axis=1, keepdims=True)
    here = lax.broadcasted_iota(jnp.int32, (1, OWN), 1).astype(F32)
    rank = jnp.where(is_shared, ahead, total + here - ahead)
    order[...] = hot(iota((OWN, OWN), 0) == rank.astype(jnp.int32))
    band_out[1] = fold(dot(order[...], pair(rotated_chunk(1 - band, 1))))
    for part in (1, 2):
        band_copy(part).start()
    turn[:, OWN:] = jnp.zeros((W, 896 - OWN), F32)
    along_rows(rank, OWN)
    column = turn[...].T[:OWN].astype(jnp.int32)
    for half in range(2):
        for at in range(0, HALF, W):
            width = min(W, HALF - at)
            back_order[half, :, at : at + width] = hot(
                iota((OWN, width), 1) + (half * HALF + at) == column[:, :width]
            )
    for j in range(2):
        now[j] = rotated_chunk(band, j)

    turn[...] = jnp.zeros_like(turn)
    turn[:, :OWN] = jnp.broadcast_to(mass[...].reshape(1, OWN), (W, OWN))
    columns = turn[...].T[:OWN]
    mass_sq[...] = columns * columns
    mass_inv[...] = 1.0 / columns
    far_sq[...] = fold(dot(pick[:EDGE], pair(mass_sq[...])))
    info_out[1] = far_sq[...]
    info_copy.start()
    for j in range(2):
        now[j] = now[j] * columns

    edge_hi[...] = jnp.zeros_like(edge_hi)
    edge_lo[...] = jnp.zeros_like(edge_lo)
    stack[...] = jnp.zeros_like(stack)
    back_in[:, :, :, GHOST:] = jnp.zeros((DEGREE, 2, 2, EDGE - GHOST, W), F32)
    ghost_in[:, :, :, GHOST:] = jnp.zeros((DEGREE, 2, 2, EDGE - GHOST, W), F32)
    stiff_pad[...] = jnp.zeros_like(stiff_pad)
    stiff_pad[:NPE, :NPE] = stiffness[...]
    slot_pad[...] = jnp.full(slot_pad.shape, -1, jnp.int32)
    drawn = slots[...]
    is_low = (drawn >= OWN) & (drawn < OWN + GHOST)
    is_high = drawn >= OWN + GHOST
    absent = ((me == 0) & is_low) | ((me == parts - 1) & is_high)
    low_at = jnp.where(core == 0, drawn, drawn + EDGE)
    high_at = jnp.where(core == 0, drawn + (EDGE - GHOST), drawn - GHOST)
    placed = jnp.where(is_low, low_at, jnp.where(is_high, high_at, drawn))
    slot_pad[:CELLS, :NPE] = jnp.where(absent, -1, placed)
    pot_pad[...] = jnp.zeros_like(pot_pad)
    pot_pad[:CELLS, :NPE] = potential[...]

    @pl.loop(0, CELLS)
    def _(c):
        at = pl.multiple_of(c * PAD, PAD)
        row = slot_pad[pl.ds(c, 1), :]
        nodes = hot(iota((ROWS, PAD), 0) == row)
        one_hot[:, pl.ds(at, PAD)] = nodes
        diagonal = iota((PAD, PAD), 0) == iota((PAD, PAD), 1)
        cell = scale[c] * stiff_pad[...] + jnp.where(diagonal, pot_pad[pl.ds(c, 1), :], 0.0)
        stacked = jnp.concatenate(split(cell), axis=0)
        for start, size, high, low, lane in (
            (0, OWN, prod_own_hi, prod_own_lo, 0),
            (OWN, EDGE, prod_edge_hi, prod_edge_lo, 0),
            (OWN + EDGE, EDGE, prod_edge_hi, prod_edge_lo, 256),
        ):
            both = dot_nt(stacked, nodes[start : start + size])
            cols = slice(lane, lane + size)
            high[pl.ds(at, PAD), cols], low[pl.ds(at, PAD), cols] = split(both[:PAD] + both[PAD:])

    def block(rows, cols, high, low):
        left = one_hot[rows, :]
        return dot(left, high[:, cols]) + dot(left, low[:, cols])

    def own_block(at):
        end = min(at + 256, OWN)
        whole = block(slice(at, OWN), slice(at, end), prod_own_hi, prod_own_lo)
        own_hi[at:OWN, at:end], own_lo[at:OWN, at:end] = split(whole)
        if end < OWN:
            own_hi[at:end, end:], own_lo[at:end, end:] = split(whole[end - at :].T)

    def edge_rows(at):
        end = min(at + 256, OWN)
        whole = block(slice(OWN, ROWS), slice(at, end), prod_own_hi, prod_own_lo)
        own_hi[OWN:, at:end], own_lo[OWN:, at:end] = split(whole)
        for edge in (FAR, NEAR):
            cols = slice((edge + 1) * 256, (edge + 1) * 256 + EDGE)
            flipped = whole[edge * EDGE : (edge + 1) * EDGE].T
            edge_hi[at:end, cols], edge_lo[at:end, cols] = split(flipped)

    def edge_block():
        for edge in (FAR, NEAR):
            cols = slice(edge * 256, edge * 256 + EDGE)
            to = slice((edge + 1) * 256, (edge + 1) * 256 + EDGE)
            square = block(slice(OWN, ROWS), cols, prod_edge_hi, prod_edge_lo)
            edge_hi[OWN:, to], edge_lo[OWN:, to] = split(square)

    def far_columns():
        edge_hi[:, :EDGE] = dot(own_hi[...], place[FAR]).astype(BF16)
        edge_lo[:, :EDGE] = dot(own_lo[...], place[FAR]).astype(BF16)

    def begin(j):
        ghost_out[0, j] = fold(dot(pick[...], pair(now[j])))
        ghost_copy(0, j, FAR).start()
        ghost_copy(0, j, NEAR).start()

    def begin_whole():
        band_copy(0).wait_recv()
        now[0] = now[0] + mass_cols() * band_in[0]
        own_pair[0] = pair(now[0])
        begin(0)

    def begin_half(half):
        band_copy(1 + half).wait_recv()
        arrived = pair(band_in[1, half * HALF : (half + 1) * HALF])
        now[1] = now[1] + mass_cols() * fold(dot(back_order[half], arrived))
        if half == 0:
            begin(1)
        else:
            own_pair[1] = pair(now[1])

    def mass_cols():
        return mass_sq[...] * mass_inv[...]

    def own_product(j):
        pre[j] = apply_pair(own_hi[...], own_lo[...], own_pair[j])

    def contribute(k, j):
        for edge in (NEAR, FAR):
            ghost_copy(k, j, edge).wait_recv()
        far_ghost = ghost_in[k, j, FAR]
        if k > 0:
            far_ghost = far_ghost + COEFS[k - 1][0] * echo[j]
        stack[j, 256 : 256 + EDGE] = far_ghost
        stack[j, 512 : 512 + EDGE] = ghost_in[k, j, NEAR]
        start = 0 if k > 0 else 256
        packed = pair(stack[j, start:])
        stack_pair[j, start:] = packed
        back_out[k, j] = pre[j, OWN:] + apply_pair(
            edge_hi[OWN:, start:], edge_lo[OWN:, start:], packed
        )
        back_copy(k, j, NEAR).start()
        back_copy(k, j, FAR).start()

    def gather_own(k, j):
        start = 0 if k > 0 else 256
        acc[j] = pre[j, :OWN] + apply_pair(
            edge_hi[:OWN, start:], edge_lo[:OWN, start:], stack_pair[j, start:]
        )
        if k < DEGREE - 1:
            echo[j] = info_in[1] * fold(dot(same[...], pair(back_out[k, j, :EDGE])))

    def settle_chip(k, j):
        back_copy(k, j, NEAR).wait_recv()
        front, past = COEFS[k]
        raw = acc[j] + fold(dot(place[NEAR], pair(back_in[k, j, NEAR])))
        current = now[j]
        following = front * (mass_sq[...] * raw - centre * current)
        if k > 0:
            following = following - past * before[j]
        packed = pair(following)
        own_pair[j] = packed
        ghost_out[k + 1, j, :EDGE] = fold(dot(pick[:EDGE], packed))
        ghost_copy(k + 1, j, FAR).start()
        before[j] = current
        now[j] = following

    def settle_far(k, j):
        back_copy(k, j, FAR).wait_recv()
        change = COEFS[k][0] * far_sq[...] * back_in[k, j, FAR]
        stack[j, :EDGE] = change
        following = now[j] + fold(dot(place[FAR], pair(change)))
        ghost_out[k + 1, j, EDGE:] = fold(dot(pick[EDGE:], pair(following)))
        ghost_copy(k + 1, j, NEAR).start()
        now[j] = following

    def finish(j):
        last = DEGREE - 1
        back_copy(last, j, NEAR).wait_recv()
        raw = acc[j] + fold(dot(place[NEAR], pair(back_in[last, j, NEAR])))
        front, past = COEFS[last]
        rest = centre * now[j] + (past / front) * before[j]
        back_copy(last, j, FAR).wait_recv()
        raw = raw + fold(dot(place[FAR], pair(back_in[last, j, FAR])))
        out[:, j * W : (j + 1) * W] = mass_inv[...] * (mass_sq[...] * raw - rest)

    own_block(0)
    own_block(256)
    own_block(512)
    own_block(768)
    begin_whole()
    for at in range(0, OWN, 256):
        edge_rows(at)
    edge_block()
    info_copy.wait_recv()
    theirs = info_in[0]
    turn[:, :256] = jnp.concatenate([theirs, jnp.zeros((256 - EDGE, W), F32)], axis=0).T
    same[...] = hot(
        jnp.concatenate([theirs, theirs[:, : EDGE - W]], axis=1) == turn[0:1, :EDGE]
    )
    own_product(0)
    begin_half(0)
    contribute(0, 0)
    gather_own(0, 0)
    settle_chip(0, 0)
    own_product(0)
    begin_half(1)
    own_product(1)
    contribute(0, 1)
    settle_far(0, 0)
    gather_own(0, 1)
    settle_chip(0, 1)
    own_product(1)
    far_columns()
    contribute(1, 0)
    settle_far(0, 1)
    gather_own(1, 0)
    settle_chip(1, 0)
    contribute(1, 1)
    gather_own(1, 1)
    settle_chip(1, 1)
    own_product(1)
    settle_far(1, 0)
    own_product(0)
    contribute(2, 0)
    settle_far(1, 1)
    contribute(2, 1)
    gather_own(2, 1)
    gather_own(2, 0)
    finish(0)
    finish(1)

    info_copy.wait_send()
    for part in range(3):
        band_copy(part).wait_send()

    @pl.loop(0, DEGREE)
    def _(k):
        for j in range(2):
            for edge in (FAR, NEAR):
                ghost_copy(k, j, edge).wait_send()
                back_copy(k, j, edge).wait_send()


def solution(mesh):
    parts = mesh.shape["mesh"]
    vmem = pl.BlockSpec(memory_space=pltpu.VMEM)
    smem = pl.BlockSpec(memory_space=pltpu.SMEM)
    hbm = pl.BlockSpec(memory_space=pltpu.HBM)
    dma = pltpu.SemaphoreType.DMA

    def body(states, mass, stiffness, scale, potential, slots, shared, coefficients):
        def run(*refs):
            kernel(parts, *refs)

        filtered = pl.pallas_call(
            run,
            out_shape=jax.ShapeDtypeStruct((OWN, BANDW), F32),
            in_specs=[hbm, hbm, hbm, smem, hbm, hbm, hbm, hbm],
            out_specs=vmem,
            scratch_shapes=[
                pltpu.VMEM(states.shape, F32),
                pltpu.VMEM(coefficients.shape, F32),
                pltpu.VMEM(shared.shape, jnp.int32),
                pltpu.VMEM(mass.shape, F32),
                pltpu.VMEM(stiffness.shape, F32),
                pltpu.VMEM(potential.shape, F32),
                pltpu.VMEM(slots.shape, jnp.int32),
                dma((7,)),
                pltpu.VMEM((PAD, PAD), F32),
                pltpu.VMEM((8, PAD), jnp.int32),
                pltpu.VMEM((8, PAD), F32),
                pltpu.VMEM((8, 256), jnp.int32),
                pltpu.VMEM((W, 896), F32),
                pltpu.VMEM((OWN, W), F32),
                pltpu.VMEM((OWN, W), F32),
                pltpu.VMEM((EDGE, W), F32),
                pltpu.VMEM((ROWS, CELLS * PAD), BF16),
                pltpu.VMEM((CELLS * PAD, OWN), BF16),
                pltpu.VMEM((CELLS * PAD, OWN), BF16),
                pltpu.VMEM((CELLS * PAD, 512), BF16),
                pltpu.VMEM((CELLS * PAD, 512), BF16),
                pltpu.VMEM((ROWS, OWN), BF16),
                pltpu.VMEM((ROWS, OWN), BF16),
                pltpu.VMEM((ROWS, 768), BF16),
                pltpu.VMEM((ROWS, 768), BF16),
                pltpu.VMEM((BOTH, OWN), BF16),
                pltpu.VMEM((2, OWN, EDGE), BF16),
                pltpu.VMEM((EDGE, EDGE), BF16),
                pltpu.VMEM((OWN, OWN), BF16),
                pltpu.VMEM((2, OWN, HALF), BF16),
                pltpu.VMEM((2, EDGE, W), F32),
                pltpu.VMEM((2, EDGE, W), F32),
                pltpu.VMEM((2, OWN, W), F32),
                pltpu.VMEM((2, OWN, W), F32),
                pltpu.VMEM((2, OWN, W), F32),
                pltpu.VMEM((2, OWN, W), F32),
                pltpu.VMEM((2, ROWS, W), F32),
                pltpu.VMEM((2, OWN, W), F32),
                pltpu.VMEM((2, 768, W), F32),
                pltpu.VMEM((2, 768, 2 * W), BF16),
                pltpu.VMEM((2, OWN, 2 * W), BF16),
                pltpu.VMEM((2, EDGE, W), F32),
                pltpu.VMEM((DEGREE, 2, BOTH, W), F32),
                pltpu.VMEM((DEGREE, 2, 2, EDGE, W), F32),
                pltpu.VMEM((DEGREE, 2, BOTH, W), F32),
                pltpu.VMEM((DEGREE, 2, 2, EDGE, W), F32),
                dma((2,)),
                dma((3,)),
                dma((3,)),
                dma((DEGREE, 2, 2)),
                dma((DEGREE, 2, 2)),
                dma((DEGREE, 2, 2)),
                dma((DEGREE, 2, 2)),
            ],
            compiler_params=pltpu.CompilerParams(
                collective_id=0, has_side_effects=True, vmem_limit_bytes=56 * 2**20
            ),
        )(states, mass, stiffness, scale, potential, slots, shared, coefficients)
        return filtered * COEFS[-1][0]

    return jax.shard_map(
        body,
        mesh=mesh,
        in_specs=(
            P("mesh", "band"),
            P("mesh"),
            P(),
            P("mesh"),
            P("mesh", None),
            P("mesh", None),
            P("mesh", None, None),
            P("band", None),
        ),
        out_specs=P("mesh", "band"),
        check_vma=False,
    )
```

```python
import jax
import jax.numpy as jnp
from jax import lax
from jax.experimental import pallas as pl
from jax.experimental.pallas import tpu as pltpu
from jax.sharding import PartitionSpec as P

MESH = pl.DeviceIdType.MESH
F32, BF16 = jnp.float32, jnp.bfloat16

DEGREE = 3
OWN = 864
GHOST = 216
EDGE = 224
HALF = OWN // 2
BOTH = 2 * EDGE
ROWS = OWN + BOTH
NPE = 343
PAD = 384
KEEP = 352
CELLS = 4
W = 128
BANDW = 256
FAR, NEAR = 0, 1

low_end = -3.0
low_bound = 2.0
high_bound = 14.0

half_span = (high_bound - low_bound) / 2.0
centre = (high_bound + low_bound) / 2.0
sigma_first = half_span / (low_end - centre)
gamma_term = 2.0 / sigma_first


def chebyshev():
    rows = [(sigma_first / half_span, 0.0)]
    now = sigma_first
    for _ in range(DEGREE - 1):
        later = 1.0 / (gamma_term - now)
        rows.append((2.0 * later / half_span, now * later))
        now = later
    return rows


COEFS = chebyshev()


def dot(a, b):
    return jnp.dot(a, b, preferred_element_type=F32)


def dot_nt(a, b):
    return lax.dot_general(a, b, (((1,), (1,)), ((), ())), preferred_element_type=F32)


def split(x):
    high = x.astype(BF16)
    return high, (x - high.astype(F32)).astype(BF16)


def pair(x):
    return jnp.concatenate(split(x), axis=1)


def fold(y):
    return y[:, :W] + y[:, W:]


def apply_pair(high, low, packed):
    return fold(dot(high, packed)) + dot(low, packed[:, :W])


def iota(shape, dim):
    return lax.broadcasted_iota(jnp.int32, shape, dim)


def hot(mask):
    return jnp.where(mask, 1.0, 0.0).astype(BF16)


def kernel(
    parts,
    states_at,
    mass_at,
    stiffness_at,
    scale,
    potential_at,
    slots_at,
    shared_at,
    coefficients_at,
    out,
    states,
    coefficients,
    shared,
    mass,
    stiffness,
    potential,
    slots,
    load_sems,
    stiff_pad,
    slot_pad,
    pot_pad,
    list_pad,
    turn,
    mass_sq,
    mass_inv,
    far_sq,
    one_hot,
    prod_own_hi,
    prod_own_lo,
    prod_edge_hi,
    prod_edge_lo,
    own_hi,
    own_lo,
    edge_hi,
    edge_lo,
    pick,
    place,
    same,
    order,
    back_order,
    info_out,
    info_in,
    band_out,
    band_in,
    now,
    before,
    pre,
    acc,
    stack,
    stack_pair,
    own_pair,
    echo,
    ghost_out,
    ghost_in,
    back_out,
    back_in,
    info_sems,
    band_send,
    band_recv,
    ghost_send,
    ghost_recv,
    back_send,
    back_recv,
):
    me = lax.axis_index("mesh")
    band = lax.axis_index("band")
    loads = [
        pltpu.make_async_copy(source, target, load_sems.at[at])
        for at, (source, target) in enumerate(
            (
                (states_at, states),
                (coefficients_at, coefficients),
                (shared_at, shared),
                (mass_at, mass),
                (stiffness_at, stiffness),
                (potential_at, potential),
                (slots_at, slots),
            )
        )
    ]
    for load in loads:
        load.start()

    core = lax.rem(me, 2)
    near = (me + 1 - 2 * core, band)
    far = (lax.rem(me + parts - 1 + 2 * core, parts), band)
    other = (me, 1 - band)

    barrier = pltpu.get_barrier_semaphore()
    for device in (other, far, near):
        pl.semaphore_signal(barrier, inc=1, device_id=device, device_id_type=MESH)

    def band_copy(part):
        piece = (0,) if part == 0 else (1, pl.ds((part - 1) * HALF, HALF))
        return pltpu.make_async_remote_copy(
            src_ref=band_out.at[piece],
            dst_ref=band_in.at[piece],
            send_sem=band_send.at[part],
            recv_sem=band_recv.at[part],
            device_id=other,
            device_id_type=MESH,
        )

    def chain_copy(src, dst, send, recv, k, j, edge):
        return pltpu.make_async_remote_copy(
            src_ref=src.at[k, j, pl.ds(edge * EDGE, GHOST)],
            dst_ref=dst.at[k, j, edge, pl.ds(0, GHOST)],
            send_sem=send.at[k, j, edge],
            recv_sem=recv.at[k, j, edge],
            device_id=far if edge == FAR else near,
            device_id_type=MESH,
        )

    def ghost_copy(k, j, edge):
        return chain_copy(ghost_out, ghost_in, ghost_send, ghost_recv, k, j, edge)

    def back_copy(k, j, edge):
        return chain_copy(back_out, back_in, back_send, back_recv, k, j, edge)

    info_copy = pltpu.make_async_remote_copy(
        src_ref=info_out,
        dst_ref=info_in,
        send_sem=info_sems.at[0],
        recv_sem=info_sems.at[1],
        device_id=far,
        device_id_type=MESH,
    )

    loads[0].wait()
    loads[1].wait()
    x_hi, x_lo = split(states[...])

    def rotated_chunk(which, j):
        at = pl.multiple_of(which * BANDW + j * W, W)
        c_hi, c_lo = split(coefficients[:, pl.ds(at, W)])
        return fold(dot(x_hi, jnp.concatenate([c_hi, c_lo], axis=1))) + dot(x_lo, c_hi)

    band_out[0] = rotated_chunk(1 - band, 0)
    pl.semaphore_wait(barrier, 3)
    band_copy(0).start()

    for load in loads[2:]:
        load.wait()
    list_pad[...] = jnp.full(list_pad.shape, -1, jnp.int32)
    first, second = shared[0, 0:1, :], shared[0, 1:2, :]
    list_pad[0:1, :GHOST] = jnp.where(core == 0, first, second)
    list_pad[1:2, :GHOST] = jnp.where(core == 0, second, first)

    def along_rows(row, length):
        turn[:, :length] = jnp.broadcast_to(row.astype(F32), (W, length))

    for edge in (FAR, NEAR):
        row = list_pad[edge : edge + 1, :]
        place[edge] = hot(iota((OWN, EDGE), 0) == row[:, :EDGE])
        along_rows(row, 256)
        column = turn[:, :256].T[:EDGE]
        if edge == FAR:
            info_out[0] = column
        column = column.astype(jnp.int32)
        for at in range(0, OWN, W):
            width = min(W, OWN - at)
            pick[edge * EDGE : (edge + 1) * EDGE, at : at + width] = hot(
                iota((EDGE, width), 1) + at == column[:, :width]
            )

    counts = dot(jnp.ones((16, BOTH), BF16), pick[...])
    is_shared = counts > 0.5
    ahead = dot(hot(is_shared), hot(iota((OWN, OWN), 0) < iota((OWN, OWN), 1)))[0:1]
    is_shared = is_shared[0:1]
    total = jnp.sum(jnp.where(is_shared, 1.0, 0.0), axis=1, keepdims=True)
    here = lax.broadcasted_iota(jnp.int32, (1, OWN), 1).astype(F32)
    rank = jnp.where(is_shared, ahead, total + here - ahead)
    order[...] = hot(iota((OWN, OWN), 0) == rank.astype(jnp.int32))
    band_out[1] = fold(dot(order[...], pair(rotated_chunk(1 - band, 1))))
    for part in (1, 2):
        band_copy(part).start()
    turn[:, OWN:] = jnp.zeros((W, 896 - OWN), F32)
    along_rows(rank, OWN)
    column = turn[...].T[:OWN].astype(jnp.int32)
    for half in range(2):
        for at in range(0, HALF, W):
            width = min(W, HALF - at)
            back_order[half, :, at : at + width] = hot(
                iota((OWN, width), 1) + (half * HALF + at) == column[:, :width]
            )
    for j in range(2):
        now[j] = rotated_chunk(band, j)

    turn[...] = jnp.zeros_like(turn)
    turn[:, :OWN] = jnp.broadcast_to(mass[...].reshape(1, OWN), (W, OWN))
    columns = turn[...].T[:OWN]
    mass_sq[...] = columns * columns
    mass_inv[...] = 1.0 / columns
    far_sq[...] = fold(dot(pick[:EDGE], pair(mass_sq[...])))
    info_out[1] = far_sq[...]
    info_copy.start()
    for j in range(2):
        now[j] = now[j] * columns

    edge_hi[...] = jnp.zeros_like(edge_hi)
    edge_lo[...] = jnp.zeros_like(edge_lo)
    stack[...] = jnp.zeros_like(stack)
    back_in[:, :, :, GHOST:] = jnp.zeros((DEGREE, 2, 2, EDGE - GHOST, W), F32)
    ghost_in[:, :, :, GHOST:] = jnp.zeros((DEGREE, 2, 2, EDGE - GHOST, W), F32)
    stiff_pad[...] = jnp.zeros_like(stiff_pad)
    stiff_pad[:NPE, :NPE] = stiffness[...]
    slot_pad[...] = jnp.full(slot_pad.shape, -1, jnp.int32)
    drawn = slots[...]
    is_low = (drawn >= OWN) & (drawn < OWN + GHOST)
    is_high = drawn >= OWN + GHOST
    absent = ((me == 0) & is_low) | ((me == parts - 1) & is_high)
    low_at = jnp.where(core == 0, drawn, drawn + EDGE)
    high_at = jnp.where(core == 0, drawn + (EDGE - GHOST), drawn - GHOST)
    placed = jnp.where(is_low, low_at, jnp.where(is_high, high_at, drawn))
    slot_pad[:CELLS, :NPE] = jnp.where(absent, -1, placed)
    pot_pad[...] = jnp.zeros_like(pot_pad)
    pot_pad[:CELLS, :NPE] = potential[...]

    @pl.loop(0, CELLS)
    def _(c):
        at = pl.multiple_of(c * PAD, PAD)
        row = slot_pad[pl.ds(c, 1), :]
        nodes = hot(iota((ROWS, PAD), 0) == row)
        one_hot[:, pl.ds(at, PAD)] = nodes
        diagonal = iota((KEEP, PAD), 0) == iota((KEEP, PAD), 1)
        cell = scale[c] * stiff_pad[:KEEP] + jnp.where(diagonal, pot_pad[pl.ds(c, 1), :], 0.0)
        stacked = jnp.concatenate(split(cell), axis=0)
        for start, size, high, low, lane in (
            (0, OWN, prod_own_hi, prod_own_lo, 0),
            (OWN, EDGE, prod_edge_hi, prod_edge_lo, 0),
            (OWN + EDGE, EDGE, prod_edge_hi, prod_edge_lo, 256),
        ):
            both = dot_nt(stacked, nodes[start : start + size])
            cols = slice(lane, lane + size)
            total_rows = both[:KEEP] + both[KEEP:]
            high[pl.ds(at, KEEP), cols], low[pl.ds(at, KEEP), cols] = split(total_rows)
            spare = pl.ds(pl.multiple_of(at + KEEP, 32), PAD - KEEP)
            for to in (high, low):
                to[spare, cols] = jnp.zeros((PAD - KEEP, size), BF16)

    def block(rows, cols, high, low):
        left = one_hot[rows, :]
        return dot(left, high[:, cols]) + dot(left, low[:, cols])

    def own_block(at):
        end = min(at + 256, OWN)
        whole = block(slice(at, OWN), slice(at, end), prod_own_hi, prod_own_lo)
        own_hi[at:OWN, at:end], own_lo[at:OWN, at:end] = split(whole)
        if end < OWN:
            own_hi[at:end, end:], own_lo[at:end, end:] = split(whole[end - at :].T)

    def edge_rows(at):
        end = min(at + 256, OWN)
        whole = block(slice(OWN, ROWS), slice(at, end), prod_own_hi, prod_own_lo)
        own_hi[OWN:, at:end], own_lo[OWN:, at:end] = split(whole)
        for edge in (FAR, NEAR):
            cols = slice((edge + 1) * 256, (edge + 1) * 256 + EDGE)
            flipped = whole[edge * EDGE : (edge + 1) * EDGE].T
            edge_hi[at:end, cols], edge_lo[at:end, cols] = split(flipped)

    def edge_block():
        for edge in (FAR, NEAR):
            cols = slice(edge * 256, edge * 256 + EDGE)
            to = slice((edge + 1) * 256, (edge + 1) * 256 + EDGE)
            square = block(slice(OWN, ROWS), cols, prod_edge_hi, prod_edge_lo)
            edge_hi[OWN:, to], edge_lo[OWN:, to] = split(square)

    def far_columns():
        edge_hi[:, :EDGE] = dot(own_hi[...], place[FAR]).astype(BF16)
        edge_lo[:, :EDGE] = dot(own_lo[...], place[FAR]).astype(BF16)

    def begin(j):
        ghost_out[0, j] = fold(dot(pick[...], pair(now[j])))
        ghost_copy(0, j, FAR).start()
        ghost_copy(0, j, NEAR).start()

    def begin_whole():
        band_copy(0).wait_recv()
        now[0] = now[0] + mass_cols() * band_in[0]
        own_pair[0] = pair(now[0])
        begin(0)

    def begin_half(half):
        band_copy(1 + half).wait_recv()
        arrived = pair(band_in[1, half * HALF : (half + 1) * HALF])
        now[1] = now[1] + mass_cols() * fold(dot(back_order[half], arrived))
        if half == 0:
            begin(1)
        else:
            own_pair[1] = pair(now[1])

    def mass_cols():
        return mass_sq[...] * mass_inv[...]

    def own_product(j):
        pre[j] = apply_pair(own_hi[...], own_lo[...], own_pair[j])

    def contribute(k, j):
        for edge in (NEAR, FAR):
            ghost_copy(k, j, edge).wait_recv()
        far_ghost = ghost_in[k, j, FAR]
        if k > 0:
            far_ghost = far_ghost + COEFS[k - 1][0] * echo[j]
        stack[j, 256 : 256 + EDGE] = far_ghost
        stack[j, 512 : 512 + EDGE] = ghost_in[k, j, NEAR]
        start = 0 if k > 0 else 256
        packed = pair(stack[j, start:])
        stack_pair[j, start:] = packed
        back_out[k, j] = pre[j, OWN:] + apply_pair(
            edge_hi[OWN:, start:], edge_lo[OWN:, start:], packed
        )
        back_copy(k, j, NEAR).start()
        back_copy(k, j, FAR).start()

    def gather_own(k, j):
        start = 0 if k > 0 else 256
        acc[j] = pre[j, :OWN] + apply_pair(
            edge_hi[:OWN, start:], edge_lo[:OWN, start:], stack_pair[j, start:]
        )
        if k < DEGREE - 1:
            echo[j] = info_in[1] * fold(dot(same[...], pair(back_out[k, j, :EDGE])))

    def settle_chip(k, j):
        back_copy(k, j, NEAR).wait_recv()
        front, past = COEFS[k]
        raw = acc[j] + fold(dot(place[NEAR], pair(back_in[k, j, NEAR])))
        current = now[j]
        following = front * (mass_sq[...] * raw - centre * current)
        if k > 0:
            following = following - past * before[j]
        packed = pair(following)
        own_pair[j] = packed
        ghost_out[k + 1, j, :EDGE] = fold(dot(pick[:EDGE], packed))
        ghost_copy(k + 1, j, FAR).start()
        before[j] = current
        now[j] = following

    def settle_far(k, j):
        back_copy(k, j, FAR).wait_recv()
        change = COEFS[k][0] * far_sq[...] * back_in[k, j, FAR]
        stack[j, :EDGE] = change
        following = now[j] + fold(dot(place[FAR], pair(change)))
        ghost_out[k + 1, j, EDGE:] = fold(dot(pick[EDGE:], pair(following)))
        ghost_copy(k + 1, j, NEAR).start()
        now[j] = following

    def finish(j):
        last = DEGREE - 1
        back_copy(last, j, NEAR).wait_recv()
        raw = acc[j] + fold(dot(place[NEAR], pair(back_in[last, j, NEAR])))
        front, past = COEFS[last]
        rest = centre * now[j] + (past / front) * before[j]
        back_copy(last, j, FAR).wait_recv()
        raw = raw + fold(dot(place[FAR], pair(back_in[last, j, FAR])))
        out[:, j * W : (j + 1) * W] = mass_inv[...] * (mass_sq[...] * raw - rest)

    for at in range(0, OWN, 256):
        edge_rows(at)
    edge_block()
    for at in range(0, OWN, 256):
        own_block(at)
    begin_whole()
    own_product(0)
    far_columns()
    info_copy.wait_recv()
    theirs = info_in[0]
    turn[:, :256] = jnp.concatenate([theirs, jnp.zeros((256 - EDGE, W), F32)], axis=0).T
    same[...] = hot(
        jnp.concatenate([theirs, theirs[:, : EDGE - W]], axis=1) == turn[0:1, :EDGE]
    )
    begin_half(0)
    contribute(0, 0)
    gather_own(0, 0)
    settle_chip(0, 0)
    begin_half(1)
    own_product(1)
    contribute(0, 1)
    gather_own(0, 1)
    settle_far(0, 0)
    settle_chip(0, 1)
    own_product(0)
    own_product(1)
    contribute(1, 0)
    settle_far(0, 1)
    gather_own(1, 0)
    settle_chip(1, 0)
    contribute(1, 1)
    gather_own(1, 1)
    settle_chip(1, 1)
    settle_far(1, 0)
    own_product(0)
    contribute(2, 0)
    settle_far(1, 1)
    own_product(1)
    contribute(2, 1)
    gather_own(2, 1)
    gather_own(2, 0)
    finish(0)
    finish(1)

    info_copy.wait_send()
    for part in range(3):
        band_copy(part).wait_send()

    @pl.loop(0, DEGREE)
    def _(k):
        for j in range(2):
            for edge in (FAR, NEAR):
                ghost_copy(k, j, edge).wait_send()
                back_copy(k, j, edge).wait_send()


def solution(mesh):
    parts = mesh.shape["mesh"]
    vmem = pl.BlockSpec(memory_space=pltpu.VMEM)
    smem = pl.BlockSpec(memory_space=pltpu.SMEM)
    hbm = pl.BlockSpec(memory_space=pltpu.HBM)
    dma = pltpu.SemaphoreType.DMA

    def body(states, mass, stiffness, scale, potential, slots, shared, coefficients):
        def run(*refs):
            kernel(parts, *refs)

        filtered = pl.pallas_call(
            run,
            out_shape=jax.ShapeDtypeStruct((OWN, BANDW), F32),
            in_specs=[hbm, hbm, hbm, smem, hbm, hbm, hbm, hbm],
            out_specs=vmem,
            scratch_shapes=[
                pltpu.VMEM(states.shape, F32),
                pltpu.VMEM(coefficients.shape, F32),
                pltpu.VMEM(shared.shape, jnp.int32),
                pltpu.VMEM(mass.shape, F32),
                pltpu.VMEM(stiffness.shape, F32),
                pltpu.VMEM(potential.shape, F32),
                pltpu.VMEM(slots.shape, jnp.int32),
                dma((7,)),
                pltpu.VMEM((PAD, PAD), F32),
                pltpu.VMEM((8, PAD), jnp.int32),
                pltpu.VMEM((8, PAD), F32),
                pltpu.VMEM((8, 256), jnp.int32),
                pltpu.VMEM((W, 896), F32),
                pltpu.VMEM((OWN, W), F32),
                pltpu.VMEM((OWN, W), F32),
                pltpu.VMEM((EDGE, W), F32),
                pltpu.VMEM((ROWS, CELLS * PAD), BF16),
                pltpu.VMEM((CELLS * PAD, OWN), BF16),
                pltpu.VMEM((CELLS * PAD, OWN), BF16),
                pltpu.VMEM((CELLS * PAD, 512), BF16),
                pltpu.VMEM((CELLS * PAD, 512), BF16),
                pltpu.VMEM((ROWS, OWN), BF16),
                pltpu.VMEM((ROWS, OWN), BF16),
                pltpu.VMEM((ROWS, 768), BF16),
                pltpu.VMEM((ROWS, 768), BF16),
                pltpu.VMEM((BOTH, OWN), BF16),
                pltpu.VMEM((2, OWN, EDGE), BF16),
                pltpu.VMEM((EDGE, EDGE), BF16),
                pltpu.VMEM((OWN, OWN), BF16),
                pltpu.VMEM((2, OWN, HALF), BF16),
                pltpu.VMEM((2, EDGE, W), F32),
                pltpu.VMEM((2, EDGE, W), F32),
                pltpu.VMEM((2, OWN, W), F32),
                pltpu.VMEM((2, OWN, W), F32),
                pltpu.VMEM((2, OWN, W), F32),
                pltpu.VMEM((2, OWN, W), F32),
                pltpu.VMEM((2, ROWS, W), F32),
                pltpu.VMEM((2, OWN, W), F32),
                pltpu.VMEM((2, 768, W), F32),
                pltpu.VMEM((2, 768, 2 * W), BF16),
                pltpu.VMEM((2, OWN, 2 * W), BF16),
                pltpu.VMEM((2, EDGE, W), F32),
                pltpu.VMEM((DEGREE, 2, BOTH, W), F32),
                pltpu.VMEM((DEGREE, 2, 2, EDGE, W), F32),
                pltpu.VMEM((DEGREE, 2, BOTH, W), F32),
                pltpu.VMEM((DEGREE, 2, 2, EDGE, W), F32),
                dma((2,)),
                dma((3,)),
                dma((3,)),
                dma((DEGREE, 2, 2)),
                dma((DEGREE, 2, 2)),
                dma((DEGREE, 2, 2)),
                dma((DEGREE, 2, 2)),
            ],
            compiler_params=pltpu.CompilerParams(
                collective_id=0, has_side_effects=True, vmem_limit_bytes=56 * 2**20
            ),
        )(states, mass, stiffness, scale, potential, slots, shared, coefficients)
        return filtered * COEFS[-1][0]

    return jax.shard_map(
        body,
        mesh=mesh,
        in_specs=(
            P("mesh", "band"),
            P("mesh"),
            P(),
            P("mesh"),
            P("mesh", None),
            P("mesh", None),
            P("mesh", None, None),
            P("band", None),
        ),
        out_specs=P("mesh", "band"),
        check_vma=False,
    )
```

```python
import jax
import jax.numpy as jnp
from jax import lax
from jax.experimental import pallas as pl
from jax.experimental.pallas import tpu as pltpu
from jax.sharding import PartitionSpec as P

MESH = pl.DeviceIdType.MESH
F32, BF16 = jnp.float32, jnp.bfloat16

DEGREE = 3
OWN = 864
GHOST = 216
EDGE = 224
HALF = OWN // 2
BOTH = 2 * EDGE
ROWS = OWN + BOTH
NPE = 343
PAD = 384
KEEP = 352
CELLS = 4
W = 128
BANDW = 256
FAR, NEAR = 0, 1

low_end = -3.0
low_bound = 2.0
high_bound = 14.0

half_span = (high_bound - low_bound) / 2.0
centre = (high_bound + low_bound) / 2.0
sigma_first = half_span / (low_end - centre)
gamma_term = 2.0 / sigma_first


def chebyshev():
    rows = [(sigma_first / half_span, 0.0)]
    now = sigma_first
    for _ in range(DEGREE - 1):
        later = 1.0 / (gamma_term - now)
        rows.append((2.0 * later / half_span, now * later))
        now = later
    return rows


COEFS = chebyshev()


def dot(a, b):
    return jnp.dot(a, b, preferred_element_type=F32)


def dot_nt(a, b):
    return lax.dot_general(a, b, (((1,), (1,)), ((), ())), preferred_element_type=F32)


def split(x):
    high = x.astype(BF16)
    return high, (x - high.astype(F32)).astype(BF16)


def pair(x):
    return jnp.concatenate(split(x), axis=1)


def fold(y):
    return y[:, :W] + y[:, W:]


def apply_pair(high, low, packed):
    return fold(dot(high, packed)) + dot(low, packed[:, :W])


def iota(shape, dim):
    return lax.broadcasted_iota(jnp.int32, shape, dim)


def hot(mask):
    return jnp.where(mask, 1.0, 0.0).astype(BF16)


def kernel(
    parts,
    states_at,
    mass_at,
    stiffness_at,
    scale,
    potential_at,
    slots_at,
    shared_at,
    coefficients_at,
    out,
    states,
    coefficients,
    shared,
    mass,
    stiffness,
    potential,
    slots,
    load_sems,
    stiff_pad,
    slot_pad,
    pot_pad,
    list_pad,
    turn,
    mass_sq,
    mass_inv,
    far_sq,
    one_hot,
    prod_own_hi,
    prod_own_lo,
    prod_edge_hi,
    prod_edge_lo,
    own_hi,
    own_lo,
    edge_hi,
    edge_lo,
    pick,
    place,
    same,
    order,
    back_order,
    info_out,
    info_in,
    band_out,
    band_in,
    now,
    before,
    pre,
    acc,
    stack,
    stack_pair,
    own_pair,
    echo,
    ghost_out,
    ghost_in,
    back_out,
    back_in,
    info_sems,
    band_send,
    band_recv,
    ghost_send,
    ghost_recv,
    back_send,
    back_recv,
):
    me = lax.axis_index("mesh")
    band = lax.axis_index("band")
    loads = [
        pltpu.make_async_copy(source, target, load_sems.at[at])
        for at, (source, target) in enumerate(
            (
                (states_at, states),
                (coefficients_at, coefficients),
                (shared_at, shared),
                (mass_at, mass),
                (stiffness_at, stiffness),
                (potential_at, potential),
                (slots_at, slots),
            )
        )
    ]
    for load in loads:
        load.start()

    core = lax.rem(me, 2)
    near = (me + 1 - 2 * core, band)
    far = (lax.rem(me + parts - 1 + 2 * core, parts), band)
    other = (me, 1 - band)

    barrier = pltpu.get_barrier_semaphore()
    for device in (other, far, near):
        pl.semaphore_signal(barrier, inc=1, device_id=device, device_id_type=MESH)

    def band_copy(part):
        piece = (0,) if part == 0 else (1, pl.ds((part - 1) * HALF, HALF))
        return pltpu.make_async_remote_copy(
            src_ref=band_out.at[piece],
            dst_ref=band_in.at[piece],
            send_sem=band_send.at[part],
            recv_sem=band_recv.at[part],
            device_id=other,
            device_id_type=MESH,
        )

    def chain_copy(src, dst, send, recv, k, j, edge):
        return pltpu.make_async_remote_copy(
            src_ref=src.at[k, j, pl.ds(edge * EDGE, GHOST)],
            dst_ref=dst.at[k, j, edge, pl.ds(0, GHOST)],
            send_sem=send.at[k, j, edge],
            recv_sem=recv.at[k, j, edge],
            device_id=far if edge == FAR else near,
            device_id_type=MESH,
        )

    def ghost_copy(k, j, edge):
        return chain_copy(ghost_out, ghost_in, ghost_send, ghost_recv, k, j, edge)

    def back_copy(k, j, edge):
        return chain_copy(back_out, back_in, back_send, back_recv, k, j, edge)

    info_copy = pltpu.make_async_remote_copy(
        src_ref=info_out,
        dst_ref=info_in,
        send_sem=info_sems.at[0],
        recv_sem=info_sems.at[1],
        device_id=far,
        device_id_type=MESH,
    )

    loads[0].wait()
    loads[1].wait()
    x_hi, x_lo = split(states[...])

    def rotated_chunk(which, j):
        at = pl.multiple_of(which * BANDW + j * W, W)
        c_hi, c_lo = split(coefficients[:, pl.ds(at, W)])
        return fold(dot(x_hi, jnp.concatenate([c_hi, c_lo], axis=1))) + dot(x_lo, c_hi)

    band_out[0] = rotated_chunk(1 - band, 0)
    pl.semaphore_wait(barrier, 3)
    band_copy(0).start()

    for load in loads[2:]:
        load.wait()
    list_pad[...] = jnp.full(list_pad.shape, -1, jnp.int32)
    first, second = shared[0, 0:1, :], shared[0, 1:2, :]
    list_pad[0:1, :GHOST] = jnp.where(core == 0, first, second)
    list_pad[1:2, :GHOST] = jnp.where(core == 0, second, first)

    def along_rows(row, length):
        turn[:, :length] = jnp.broadcast_to(row.astype(F32), (W, length))

    for edge in (FAR, NEAR):
        row = list_pad[edge : edge + 1, :]
        place[edge] = hot(iota((OWN, EDGE), 0) == row[:, :EDGE])
        along_rows(row, 256)
        column = turn[:, :256].T[:EDGE]
        if edge == FAR:
            info_out[0] = column
        column = column.astype(jnp.int32)
        for at in range(0, OWN, W):
            width = min(W, OWN - at)
            pick[edge * EDGE : (edge + 1) * EDGE, at : at + width] = hot(
                iota((EDGE, width), 1) + at == column[:, :width]
            )

    counts = dot(jnp.ones((16, BOTH), BF16), pick[...])
    is_shared = counts > 0.5
    ahead = dot(hot(is_shared), hot(iota((OWN, OWN), 0) < iota((OWN, OWN), 1)))[0:1]
    is_shared = is_shared[0:1]
    total = jnp.sum(jnp.where(is_shared, 1.0, 0.0), axis=1, keepdims=True)
    here = lax.broadcasted_iota(jnp.int32, (1, OWN), 1).astype(F32)
    rank = jnp.where(is_shared, ahead, total + here - ahead)
    order[...] = hot(iota((OWN, OWN), 0) == rank.astype(jnp.int32))
    band_out[1] = fold(dot(order[...], pair(rotated_chunk(1 - band, 1))))
    for part in (1, 2):
        band_copy(part).start()
    turn[:, OWN:] = jnp.zeros((W, 896 - OWN), F32)
    along_rows(rank, OWN)
    column = turn[...].T[:OWN].astype(jnp.int32)
    for half in range(2):
        for at in range(0, HALF, W):
            width = min(W, HALF - at)
            back_order[half, :, at : at + width] = hot(
                iota((OWN, width), 1) + (half * HALF + at) == column[:, :width]
            )
    for j in range(2):
        now[j] = rotated_chunk(band, j)

    turn[...] = jnp.zeros_like(turn)
    turn[:, :OWN] = jnp.broadcast_to(mass[...].reshape(1, OWN), (W, OWN))
    columns = turn[...].T[:OWN]
    mass_sq[...] = columns * columns
    mass_inv[...] = 1.0 / columns
    far_sq[...] = fold(dot(pick[:EDGE], pair(mass_sq[...])))
    info_out[1] = far_sq[...]
    info_copy.start()
    for j in range(2):
        now[j] = now[j] * columns

    edge_hi[...] = jnp.zeros_like(edge_hi)
    edge_lo[...] = jnp.zeros_like(edge_lo)
    stack[...] = jnp.zeros_like(stack)
    back_in[:, :, :, GHOST:] = jnp.zeros((DEGREE, 2, 2, EDGE - GHOST, W), F32)
    ghost_in[:, :, :, GHOST:] = jnp.zeros((DEGREE, 2, 2, EDGE - GHOST, W), F32)
    stiff_pad[...] = jnp.zeros_like(stiff_pad)
    stiff_pad[:NPE, :NPE] = stiffness[...]
    slot_pad[...] = jnp.full(slot_pad.shape, -1, jnp.int32)
    drawn = slots[...]
    is_low = (drawn >= OWN) & (drawn < OWN + GHOST)
    is_high = drawn >= OWN + GHOST
    absent = ((me == 0) & is_low) | ((me == parts - 1) & is_high)
    low_at = jnp.where(core == 0, drawn, drawn + EDGE)
    high_at = jnp.where(core == 0, drawn + (EDGE - GHOST), drawn - GHOST)
    placed = jnp.where(is_low, low_at, jnp.where(is_high, high_at, drawn))
    slot_pad[:CELLS, :NPE] = jnp.where(absent, -1, placed)
    pot_pad[...] = jnp.zeros_like(pot_pad)
    pot_pad[:CELLS, :NPE] = potential[...]

    @pl.loop(0, CELLS)
    def _(c):
        at = pl.multiple_of(c * PAD, PAD)
        row = slot_pad[pl.ds(c, 1), :]
        nodes = hot(iota((ROWS, PAD), 0) == row)
        one_hot[:, pl.ds(at, PAD)] = nodes
        diagonal = iota((KEEP, PAD), 0) == iota((KEEP, PAD), 1)
        cell = scale[c] * stiff_pad[:KEEP] + jnp.where(diagonal, pot_pad[pl.ds(c, 1), :], 0.0)
        stacked = jnp.concatenate(split(cell), axis=0)
        for start, size, high, low, lane in (
            (0, OWN, prod_own_hi, prod_own_lo, 0),
            (OWN, EDGE, prod_edge_hi, prod_edge_lo, 0),
            (OWN + EDGE, EDGE, prod_edge_hi, prod_edge_lo, 256),
        ):
            both = dot_nt(stacked, nodes[start : start + size])
            cols = slice(lane, lane + size)
            total_rows = both[:KEEP] + both[KEEP:]
            high[pl.ds(at, KEEP), cols], low[pl.ds(at, KEEP), cols] = split(total_rows)
            spare = pl.ds(pl.multiple_of(at + KEEP, 32), PAD - KEEP)
            for to in (high, low):
                to[spare, cols] = jnp.zeros((PAD - KEEP, size), BF16)

    def block(rows, cols, high, low):
        left = one_hot[rows, :]
        return dot(left, high[:, cols]) + dot(left, low[:, cols])

    def own_block(at):
        end = min(at + 256, OWN)
        whole = block(slice(at, OWN), slice(at, end), prod_own_hi, prod_own_lo)
        own_hi[at:OWN, at:end], own_lo[at:OWN, at:end] = split(whole)
        if end < OWN:
            own_hi[at:end, end:], own_lo[at:end, end:] = split(whole[end - at :].T)

    def edge_rows(at):
        end = min(at + 256, OWN)
        whole = block(slice(OWN, ROWS), slice(at, end), prod_own_hi, prod_own_lo)
        own_hi[OWN:, at:end], own_lo[OWN:, at:end] = split(whole)
        for edge in (FAR, NEAR):
            cols = slice((edge + 1) * 256, (edge + 1) * 256 + EDGE)
            flipped = whole[edge * EDGE : (edge + 1) * EDGE].T
            edge_hi[at:end, cols], edge_lo[at:end, cols] = split(flipped)

    def edge_block():
        for edge in (FAR, NEAR):
            cols = slice(edge * 256, edge * 256 + EDGE)
            to = slice((edge + 1) * 256, (edge + 1) * 256 + EDGE)
            square = block(slice(OWN, ROWS), cols, prod_edge_hi, prod_edge_lo)
            edge_hi[OWN:, to], edge_lo[OWN:, to] = split(square)

    def far_columns():
        edge_hi[:, :EDGE] = dot(own_hi[...], place[FAR]).astype(BF16)
        edge_lo[:, :EDGE] = dot(own_lo[...], place[FAR]).astype(BF16)

    def begin(j):
        ghost_out[0, j] = fold(dot(pick[...], pair(now[j])))
        ghost_copy(0, j, FAR).start()
        ghost_copy(0, j, NEAR).start()

    def begin_whole():
        band_copy(0).wait_recv()
        now[0] = now[0] + mass_cols() * band_in[0]
        own_pair[0] = pair(now[0])
        begin(0)

    def begin_half(half):
        band_copy(1 + half).wait_recv()
        arrived = pair(band_in[1, half * HALF : (half + 1) * HALF])
        now[1] = now[1] + mass_cols() * fold(dot(back_order[half], arrived))
        if half == 0:
            begin(1)
        else:
            own_pair[1] = pair(now[1])

    def mass_cols():
        return mass_sq[...] * mass_inv[...]

    def own_product(j):
        pre[j] = apply_pair(own_hi[...], own_lo[...], own_pair[j])

    def contribute(k, j):
        for edge in (NEAR, FAR):
            ghost_copy(k, j, edge).wait_recv()
        far_ghost = ghost_in[k, j, FAR]
        if k > 0:
            far_ghost = far_ghost + COEFS[k - 1][0] * echo[j]
        stack[j, 256 : 256 + EDGE] = far_ghost
        stack[j, 512 : 512 + EDGE] = ghost_in[k, j, NEAR]
        start = 0 if k > 0 else 256
        packed = pair(stack[j, start:])
        stack_pair[j, start:] = packed
        back_out[k, j] = pre[j, OWN:] + apply_pair(
            edge_hi[OWN:, start:], edge_lo[OWN:, start:], packed
        )
        back_copy(k, j, NEAR).start()
        back_copy(k, j, FAR).start()

    def gather_own(k, j):
        start = 0 if k > 0 else 256
        acc[j] = pre[j, :OWN] + apply_pair(
            edge_hi[:OWN, start:], edge_lo[:OWN, start:], stack_pair[j, start:]
        )
        if k < DEGREE - 1:
            echo[j] = info_in[1] * fold(dot(same[...], pair(back_out[k, j, :EDGE])))

    def settle_chip(k, j):
        back_copy(k, j, NEAR).wait_recv()
        front, past = COEFS[k]
        raw = acc[j] + fold(dot(place[NEAR], pair(back_in[k, j, NEAR])))
        current = now[j]
        following = front * (mass_sq[...] * raw - centre * current)
        if k > 0:
            following = following - past * before[j]
        packed = pair(following)
        own_pair[j] = packed
        ghost_out[k + 1, j, :EDGE] = fold(dot(pick[:EDGE], packed))
        ghost_copy(k + 1, j, FAR).start()
        before[j] = current
        now[j] = following

    def settle_far(k, j):
        back_copy(k, j, FAR).wait_recv()
        change = COEFS[k][0] * far_sq[...] * back_in[k, j, FAR]
        stack[j, :EDGE] = change
        following = now[j] + fold(dot(place[FAR], pair(change)))
        ghost_out[k + 1, j, EDGE:] = fold(dot(pick[EDGE:], pair(following)))
        ghost_copy(k + 1, j, NEAR).start()
        now[j] = following

    def finish(j):
        last = DEGREE - 1
        back_copy(last, j, NEAR).wait_recv()
        raw = acc[j] + fold(dot(place[NEAR], pair(back_in[last, j, NEAR])))
        front, past = COEFS[last]
        rest = centre * now[j] + (past / front) * before[j]
        back_copy(last, j, FAR).wait_recv()
        raw = raw + fold(dot(place[FAR], pair(back_in[last, j, FAR])))
        out[:, j * W : (j + 1) * W] = mass_inv[...] * (mass_sq[...] * raw - rest)

    for at in range(0, OWN, 256):
        edge_rows(at)
    edge_block()
    for at in range(0, OWN, 256):
        own_block(at)
    begin_whole()
    own_product(0)
    far_columns()
    info_copy.wait_recv()
    theirs = info_in[0]
    turn[:, :256] = jnp.concatenate([theirs, jnp.zeros((256 - EDGE, W), F32)], axis=0).T
    same[...] = hot(
        jnp.concatenate([theirs, theirs[:, : EDGE - W]], axis=1) == turn[0:1, :EDGE]
    )
    begin_half(0)
    contribute(0, 0)
    gather_own(0, 0)
    settle_chip(0, 0)
    own_product(0)
    begin_half(1)
    own_product(1)
    contribute(0, 1)
    settle_far(0, 0)
    gather_own(0, 1)
    settle_chip(0, 1)
    own_product(1)
    contribute(1, 0)
    settle_far(0, 1)
    gather_own(1, 0)
    settle_chip(1, 0)
    contribute(1, 1)
    gather_own(1, 1)
    settle_chip(1, 1)
    own_product(1)
    settle_far(1, 0)
    own_product(0)
    contribute(2, 0)
    settle_far(1, 1)
    contribute(2, 1)
    gather_own(2, 1)
    gather_own(2, 0)
    finish(0)
    finish(1)

    info_copy.wait_send()
    for part in range(3):
        band_copy(part).wait_send()

    @pl.loop(0, DEGREE)
    def _(k):
        for j in range(2):
            for edge in (FAR, NEAR):
                ghost_copy(k, j, edge).wait_send()
                back_copy(k, j, edge).wait_send()


def solution(mesh):
    parts = mesh.shape["mesh"]
    vmem = pl.BlockSpec(memory_space=pltpu.VMEM)
    smem = pl.BlockSpec(memory_space=pltpu.SMEM)
    hbm = pl.BlockSpec(memory_space=pltpu.HBM)
    dma = pltpu.SemaphoreType.DMA

    def body(states, mass, stiffness, scale, potential, slots, shared, coefficients):
        def run(*refs):
            kernel(parts, *refs)

        filtered = pl.pallas_call(
            run,
            out_shape=jax.ShapeDtypeStruct((OWN, BANDW), F32),
            in_specs=[hbm, hbm, hbm, smem, hbm, hbm, hbm, hbm],
            out_specs=vmem,
            scratch_shapes=[
                pltpu.VMEM(states.shape, F32),
                pltpu.VMEM(coefficients.shape, F32),
                pltpu.VMEM(shared.shape, jnp.int32),
                pltpu.VMEM(mass.shape, F32),
                pltpu.VMEM(stiffness.shape, F32),
                pltpu.VMEM(potential.shape, F32),
                pltpu.VMEM(slots.shape, jnp.int32),
                dma((7,)),
                pltpu.VMEM((PAD, PAD), F32),
                pltpu.VMEM((8, PAD), jnp.int32),
                pltpu.VMEM((8, PAD), F32),
                pltpu.VMEM((8, 256), jnp.int32),
                pltpu.VMEM((W, 896), F32),
                pltpu.VMEM((OWN, W), F32),
                pltpu.VMEM((OWN, W), F32),
                pltpu.VMEM((EDGE, W), F32),
                pltpu.VMEM((ROWS, CELLS * PAD), BF16),
                pltpu.VMEM((CELLS * PAD, OWN), BF16),
                pltpu.VMEM((CELLS * PAD, OWN), BF16),
                pltpu.VMEM((CELLS * PAD, 512), BF16),
                pltpu.VMEM((CELLS * PAD, 512), BF16),
                pltpu.VMEM((ROWS, OWN), BF16),
                pltpu.VMEM((ROWS, OWN), BF16),
                pltpu.VMEM((ROWS, 768), BF16),
                pltpu.VMEM((ROWS, 768), BF16),
                pltpu.VMEM((BOTH, OWN), BF16),
                pltpu.VMEM((2, OWN, EDGE), BF16),
                pltpu.VMEM((EDGE, EDGE), BF16),
                pltpu.VMEM((OWN, OWN), BF16),
                pltpu.VMEM((2, OWN, HALF), BF16),
                pltpu.VMEM((2, EDGE, W), F32),
                pltpu.VMEM((2, EDGE, W), F32),
                pltpu.VMEM((2, OWN, W), F32),
                pltpu.VMEM((2, OWN, W), F32),
                pltpu.VMEM((2, OWN, W), F32),
                pltpu.VMEM((2, OWN, W), F32),
                pltpu.VMEM((2, ROWS, W), F32),
                pltpu.VMEM((2, OWN, W), F32),
                pltpu.VMEM((2, 768, W), F32),
                pltpu.VMEM((2, 768, 2 * W), BF16),
                pltpu.VMEM((2, OWN, 2 * W), BF16),
                pltpu.VMEM((2, EDGE, W), F32),
                pltpu.VMEM((DEGREE, 2, BOTH, W), F32),
                pltpu.VMEM((DEGREE, 2, 2, EDGE, W), F32),
                pltpu.VMEM((DEGREE, 2, BOTH, W), F32),
                pltpu.VMEM((DEGREE, 2, 2, EDGE, W), F32),
                dma((2,)),
                dma((3,)),
                dma((3,)),
                dma((DEGREE, 2, 2)),
                dma((DEGREE, 2, 2)),
                dma((DEGREE, 2, 2)),
                dma((DEGREE, 2, 2)),
            ],
            compiler_params=pltpu.CompilerParams(
                collective_id=0, has_side_effects=True, vmem_limit_bytes=56 * 2**20
            ),
        )(states, mass, stiffness, scale, potential, slots, shared, coefficients)
        return filtered * COEFS[-1][0]

    return jax.shard_map(
        body,
        mesh=mesh,
        in_specs=(
            P("mesh", "band"),
            P("mesh"),
            P(),
            P("mesh"),
            P("mesh", None),
            P("mesh", None),
            P("mesh", None, None),
            P("band", None),
        ),
        out_specs=P("mesh", "band"),
        check_vma=False,
    )
```

```python
import jax
import jax.numpy as jnp
from jax import lax
from jax.experimental import pallas as pl
from jax.experimental.pallas import tpu as pltpu
from jax.sharding import PartitionSpec as P

MESH = pl.DeviceIdType.MESH
F32, BF16 = jnp.float32, jnp.bfloat16

DEGREE = 3
OWN = 864
GHOST = 216
EDGE = 224
HALF = OWN // 2
BOTH = 2 * EDGE
ROWS = OWN + BOTH
NPE = 343
PAD = 384
CELLS = 4
W = 128
BANDW = 256
FAR, NEAR = 0, 1

low_end = -3.0
low_bound = 2.0
high_bound = 14.0

half_span = (high_bound - low_bound) / 2.0
centre = (high_bound + low_bound) / 2.0
sigma_first = half_span / (low_end - centre)
gamma_term = 2.0 / sigma_first


def chebyshev():
    rows = [(sigma_first / half_span, 0.0)]
    now = sigma_first
    for _ in range(DEGREE - 1):
        later = 1.0 / (gamma_term - now)
        rows.append((2.0 * later / half_span, now * later))
        now = later
    return rows


COEFS = chebyshev()


def dot(a, b):
    return jnp.dot(a, b, preferred_element_type=F32)


def dot_nt(a, b):
    return lax.dot_general(a, b, (((1,), (1,)), ((), ())), preferred_element_type=F32)


def split(x):
    high = x.astype(BF16)
    return high, (x - high.astype(F32)).astype(BF16)


def pair(x):
    return jnp.concatenate(split(x), axis=1)


def fold(y):
    return y[:, :W] + y[:, W:]


def apply_pair(high, low, packed):
    return fold(dot(high, packed)) + dot(low, packed[:, :W])


def iota(shape, dim):
    return lax.broadcasted_iota(jnp.int32, shape, dim)


def hot(mask):
    return jnp.where(mask, 1.0, 0.0).astype(BF16)


def kernel(
    parts,
    states_at,
    mass_at,
    stiffness_at,
    scale,
    potential_at,
    slots_at,
    shared_at,
    coefficients_at,
    out,
    states,
    coefficients,
    shared,
    mass,
    stiffness,
    potential,
    slots,
    load_sems,
    stiff_pad,
    slot_pad,
    pot_pad,
    list_pad,
    turn,
    mass_sq,
    mass_inv,
    far_sq,
    one_hot,
    prod_own_hi,
    prod_own_lo,
    prod_edge_hi,
    prod_edge_lo,
    own_hi,
    own_lo,
    edge_hi,
    edge_lo,
    pick,
    place,
    same,
    order,
    back_order,
    info_out,
    info_in,
    band_out,
    band_in,
    now,
    before,
    pre,
    acc,
    stack,
    stack_pair,
    own_pair,
    echo,
    ghost_out,
    ghost_in,
    back_out,
    back_in,
    info_sems,
    band_send,
    band_recv,
    ghost_send,
    ghost_recv,
    back_send,
    back_recv,
):
    me = lax.axis_index("mesh")
    band = lax.axis_index("band")
    loads = [
        pltpu.make_async_copy(source, target, load_sems.at[at])
        for at, (source, target) in enumerate(
            (
                (states_at, states),
                (coefficients_at, coefficients),
                (shared_at, shared),
                (mass_at, mass),
                (stiffness_at, stiffness),
                (potential_at, potential),
                (slots_at, slots),
            )
        )
    ]
    for load in loads:
        load.start()

    core = lax.rem(me, 2)
    near = (me + 1 - 2 * core, band)
    far = (lax.rem(me + parts - 1 + 2 * core, parts), band)
    other = (me, 1 - band)

    barrier = pltpu.get_barrier_semaphore()
    for device in (other, far, near):
        pl.semaphore_signal(barrier, inc=1, device_id=device, device_id_type=MESH)

    def band_copy(part):
        piece = (0,) if part == 0 else (1, pl.ds((part - 1) * HALF, HALF))
        return pltpu.make_async_remote_copy(
            src_ref=band_out.at[piece],
            dst_ref=band_in.at[piece],
            send_sem=band_send.at[part],
            recv_sem=band_recv.at[part],
            device_id=other,
            device_id_type=MESH,
        )

    def chain_copy(src, dst, send, recv, k, j, edge):
        return pltpu.make_async_remote_copy(
            src_ref=src.at[k, j, pl.ds(edge * EDGE, GHOST)],
            dst_ref=dst.at[k, j, edge, pl.ds(0, GHOST)],
            send_sem=send.at[k, j, edge],
            recv_sem=recv.at[k, j, edge],
            device_id=far if edge == FAR else near,
            device_id_type=MESH,
        )

    def ghost_copy(k, j, edge):
        return chain_copy(ghost_out, ghost_in, ghost_send, ghost_recv, k, j, edge)

    def back_copy(k, j, edge):
        return chain_copy(back_out, back_in, back_send, back_recv, k, j, edge)

    info_copy = pltpu.make_async_remote_copy(
        src_ref=info_out,
        dst_ref=info_in,
        send_sem=info_sems.at[0],
        recv_sem=info_sems.at[1],
        device_id=far,
        device_id_type=MESH,
    )

    loads[0].wait()
    loads[1].wait()
    x_hi, x_lo = split(states[...])

    def rotated_chunk(which, j):
        at = pl.multiple_of(which * BANDW + j * W, W)
        c_hi, c_lo = split(coefficients[:, pl.ds(at, W)])
        return fold(dot(x_hi, jnp.concatenate([c_hi, c_lo], axis=1))) + dot(x_lo, c_hi)

    band_out[0] = rotated_chunk(1 - band, 0)
    pl.semaphore_wait(barrier, 3)
    band_copy(0).start()

    for load in loads[2:]:
        load.wait()
    list_pad[...] = jnp.full(list_pad.shape, -1, jnp.int32)
    first, second = shared[0, 0:1, :], shared[0, 1:2, :]
    list_pad[0:1, :GHOST] = jnp.where(core == 0, first, second)
    list_pad[1:2, :GHOST] = jnp.where(core == 0, second, first)

    def along_rows(row, length):
        turn[:, :length] = jnp.broadcast_to(row.astype(F32), (W, length))

    for edge in (FAR, NEAR):
        row = list_pad[edge : edge + 1, :]
        place[edge] = hot(iota((OWN, EDGE), 0) == row[:, :EDGE])
        along_rows(row, 256)
        column = turn[:, :256].T[:EDGE]
        if edge == FAR:
            info_out[0] = column
        column = column.astype(jnp.int32)
        for at in range(0, OWN, W):
            width = min(W, OWN - at)
            pick[edge * EDGE : (edge + 1) * EDGE, at : at + width] = hot(
                iota((EDGE, width), 1) + at == column[:, :width]
            )

    counts = dot(jnp.ones((16, BOTH), BF16), pick[...])
    is_shared = counts > 0.5
    ahead = dot(hot(is_shared), hot(iota((OWN, OWN), 0) < iota((OWN, OWN), 1)))[0:1]
    is_shared = is_shared[0:1]
    total = jnp.sum(jnp.where(is_shared, 1.0, 0.0), axis=1, keepdims=True)
    here = lax.broadcasted_iota(jnp.int32, (1, OWN), 1).astype(F32)
    rank = jnp.where(is_shared, ahead, total + here - ahead)
    order[...] = hot(iota((OWN, OWN), 0) == rank.astype(jnp.int32))
    band_out[1] = fold(dot(order[...], pair(rotated_chunk(1 - band, 1))))
    for part in (1, 2):
        band_copy(part).start()
    turn[:, OWN:] = jnp.zeros((W, 896 - OWN), F32)
    along_rows(rank, OWN)
    column = turn[...].T[:OWN].astype(jnp.int32)
    for half in range(2):
        for at in range(0, HALF, W):
            width = min(W, HALF - at)
            back_order[half, :, at : at + width] = hot(
                iota((OWN, width), 1) + (half * HALF + at) == column[:, :width]
            )
    for j in range(2):
        now[j] = rotated_chunk(band, j)

    turn[...] = jnp.zeros_like(turn)
    turn[:, :OWN] = jnp.broadcast_to(mass[...].reshape(1, OWN), (W, OWN))
    columns = turn[...].T[:OWN]
    mass_sq[...] = columns * columns
    mass_inv[...] = 1.0 / columns
    far_sq[...] = fold(dot(pick[:EDGE], pair(mass_sq[...])))
    info_out[1] = far_sq[...]
    info_copy.start()
    for j in range(2):
        now[j] = now[j] * columns

    edge_hi[...] = jnp.zeros_like(edge_hi)
    edge_lo[...] = jnp.zeros_like(edge_lo)
    stack[...] = jnp.zeros_like(stack)
    back_in[:, :, :, GHOST:] = jnp.zeros((DEGREE, 2, 2, EDGE - GHOST, W), F32)
    ghost_in[:, :, :, GHOST:] = jnp.zeros((DEGREE, 2, 2, EDGE - GHOST, W), F32)
    stiff_pad[...] = jnp.zeros_like(stiff_pad)
    stiff_pad[:NPE, :NPE] = stiffness[...]
    slot_pad[...] = jnp.full(slot_pad.shape, -1, jnp.int32)
    drawn = slots[...]
    is_low = (drawn >= OWN) & (drawn < OWN + GHOST)
    is_high = drawn >= OWN + GHOST
    absent = ((me == 0) & is_low) | ((me == parts - 1) & is_high)
    low_at = jnp.where(core == 0, drawn, drawn + EDGE)
    high_at = jnp.where(core == 0, drawn + (EDGE - GHOST), drawn - GHOST)
    placed = jnp.where(is_low, low_at, jnp.where(is_high, high_at, drawn))
    slot_pad[:CELLS, :NPE] = jnp.where(absent, -1, placed)
    pot_pad[...] = jnp.zeros_like(pot_pad)
    pot_pad[:CELLS, :NPE] = potential[...]

    @pl.loop(0, CELLS)
    def _(c):
        at = pl.multiple_of(c * PAD, PAD)
        row = slot_pad[pl.ds(c, 1), :]
        nodes = hot(iota((ROWS, PAD), 0) == row)
        one_hot[:, pl.ds(at, PAD)] = nodes
        diagonal = iota((PAD, PAD), 0) == iota((PAD, PAD), 1)
        cell = scale[c] * stiff_pad[...] + jnp.where(diagonal, pot_pad[pl.ds(c, 1), :], 0.0)
        stacked = jnp.concatenate(split(cell), axis=0)
        for start, size, high, low, lane in (
            (0, OWN, prod_own_hi, prod_own_lo, 0),
            (OWN, EDGE, prod_edge_hi, prod_edge_lo, 0),
            (OWN + EDGE, EDGE, prod_edge_hi, prod_edge_lo, 256),
        ):
            both = dot_nt(stacked, nodes[start : start + size])
            cols = slice(lane, lane + size)
            high[pl.ds(at, PAD), cols], low[pl.ds(at, PAD), cols] = split(both[:PAD] + both[PAD:])

    def block(rows, cols, high, low):
        left = one_hot[rows, :]
        return dot(left, high[:, cols]) + dot(left, low[:, cols])

    def own_block(at):
        end = min(at + 256, OWN)
        whole = block(slice(at, OWN), slice(at, end), prod_own_hi, prod_own_lo)
        own_hi[at:OWN, at:end], own_lo[at:OWN, at:end] = split(whole)
        if end < OWN:
            own_hi[at:end, end:], own_lo[at:end, end:] = split(whole[end - at :].T)

    def edge_rows(at):
        end = min(at + 256, OWN)
        whole = block(slice(OWN, ROWS), slice(at, end), prod_own_hi, prod_own_lo)
        own_hi[OWN:, at:end], own_lo[OWN:, at:end] = split(whole)
        for edge in (FAR, NEAR):
            cols = slice((edge + 1) * 256, (edge + 1) * 256 + EDGE)
            flipped = whole[edge * EDGE : (edge + 1) * EDGE].T
            edge_hi[at:end, cols], edge_lo[at:end, cols] = split(flipped)

    def edge_block():
        for edge in (FAR, NEAR):
            cols = slice(edge * 256, edge * 256 + EDGE)
            to = slice((edge + 1) * 256, (edge + 1) * 256 + EDGE)
            square = block(slice(OWN, ROWS), cols, prod_edge_hi, prod_edge_lo)
            edge_hi[OWN:, to], edge_lo[OWN:, to] = split(square)

    def far_columns(rows):
        edge_hi[rows, :EDGE] = dot(own_hi[rows, :], place[FAR]).astype(BF16)
        edge_lo[rows, :EDGE] = dot(own_lo[rows, :], place[FAR]).astype(BF16)

    def begin(j):
        ghost_out[0, j] = fold(dot(pick[...], pair(now[j])))
        ghost_copy(0, j, FAR).start()
        ghost_copy(0, j, NEAR).start()

    def begin_whole():
        band_copy(0).wait_recv()
        now[0] = now[0] + mass_cols() * band_in[0]
        own_pair[0] = pair(now[0])
        begin(0)

    def begin_half(half):
        band_copy(1 + half).wait_recv()
        arrived = pair(band_in[1, half * HALF : (half + 1) * HALF])
        now[1] = now[1] + mass_cols() * fold(dot(back_order[half], arrived))
        if half == 0:
            begin(1)
        else:
            own_pair[1] = pair(now[1])

    def mass_cols():
        return mass_sq[...] * mass_inv[...]

    def own_product(j):
        pre[j] = apply_pair(own_hi[...], own_lo[...], own_pair[j])

    def contribute(k, j):
        for edge in (NEAR, FAR):
            ghost_copy(k, j, edge).wait_recv()
        far_ghost = ghost_in[k, j, FAR]
        if k > 0:
            far_ghost = far_ghost + COEFS[k - 1][0] * echo[j]
        stack[j, 256 : 256 + EDGE] = far_ghost
        stack[j, 512 : 512 + EDGE] = ghost_in[k, j, NEAR]
        start = 0 if k > 0 else 256
        packed = pair(stack[j, start:])
        stack_pair[j, start:] = packed
        back_out[k, j] = pre[j, OWN:] + apply_pair(
            edge_hi[OWN:, start:], edge_lo[OWN:, start:], packed
        )
        back_copy(k, j, NEAR).start()
        back_copy(k, j, FAR).start()

    def gather_own(k, j):
        start = 0 if k > 0 else 256
        acc[j] = pre[j, :OWN] + apply_pair(
            edge_hi[:OWN, start:], edge_lo[:OWN, start:], stack_pair[j, start:]
        )
        if k < DEGREE - 1:
            echo[j] = info_in[1] * fold(dot(same[...], pair(back_out[k, j, :EDGE])))

    def settle_chip(k, j):
        back_copy(k, j, NEAR).wait_recv()
        front, past = COEFS[k]
        raw = acc[j] + fold(dot(place[NEAR], pair(back_in[k, j, NEAR])))
        current = now[j]
        following = front * (mass_sq[...] * raw - centre * current)
        if k > 0:
            following = following - past * before[j]
        packed = pair(following)
        own_pair[j] = packed
        ghost_out[k + 1, j, :EDGE] = fold(dot(pick[:EDGE], packed))
        ghost_copy(k + 1, j, FAR).start()
        before[j] = current
        now[j] = following

    def settle_far(k, j):
        back_copy(k, j, FAR).wait_recv()
        change = COEFS[k][0] * far_sq[...] * back_in[k, j, FAR]
        stack[j, :EDGE] = change
        following = now[j] + fold(dot(place[FAR], pair(change)))
        ghost_out[k + 1, j, EDGE:] = fold(dot(pick[EDGE:], pair(following)))
        ghost_copy(k + 1, j, NEAR).start()
        now[j] = following

    def finish(j):
        last = DEGREE - 1
        back_copy(last, j, NEAR).wait_recv()
        raw = acc[j] + fold(dot(place[NEAR], pair(back_in[last, j, NEAR])))
        front, past = COEFS[last]
        rest = centre * now[j] + (past / front) * before[j]
        back_copy(last, j, FAR).wait_recv()
        raw = raw + fold(dot(place[FAR], pair(back_in[last, j, FAR])))
        out[:, j * W : (j + 1) * W] = mass_inv[...] * (mass_sq[...] * raw - rest)

    own_block(0)
    own_block(256)
    own_block(512)
    own_block(768)
    far_columns(slice(0, OWN))
    begin_whole()
    for at in range(0, OWN, 256):
        edge_rows(at)
    edge_block()
    info_copy.wait_recv()
    theirs = info_in[0]
    turn[:, :256] = jnp.concatenate([theirs, jnp.zeros((256 - EDGE, W), F32)], axis=0).T
    same[...] = hot(
        jnp.concatenate([theirs, theirs[:, : EDGE - W]], axis=1) == turn[0:1, :EDGE]
    )
    own_product(0)
    begin_half(0)
    contribute(0, 0)
    gather_own(0, 0)
    settle_chip(0, 0)
    own_product(0)
    begin_half(1)
    own_product(1)
    contribute(0, 1)
    settle_far(0, 0)
    gather_own(0, 1)
    settle_chip(0, 1)
    own_product(1)
    far_columns(slice(OWN, ROWS))
    contribute(1, 0)
    settle_far(0, 1)
    gather_own(1, 0)
    settle_chip(1, 0)
    contribute(1, 1)
    gather_own(1, 1)
    settle_chip(1, 1)
    own_product(1)
    settle_far(1, 0)
    own_product(0)
    contribute(2, 0)
    settle_far(1, 1)
    contribute(2, 1)
    gather_own(2, 1)
    gather_own(2, 0)
    finish(0)
    finish(1)

    info_copy.wait_send()
    for part in range(3):
        band_copy(part).wait_send()

    @pl.loop(0, DEGREE)
    def _(k):
        for j in range(2):
            for edge in (FAR, NEAR):
                ghost_copy(k, j, edge).wait_send()
                back_copy(k, j, edge).wait_send()


def solution(mesh):
    parts = mesh.shape["mesh"]
    vmem = pl.BlockSpec(memory_space=pltpu.VMEM)
    smem = pl.BlockSpec(memory_space=pltpu.SMEM)
    hbm = pl.BlockSpec(memory_space=pltpu.HBM)
    dma = pltpu.SemaphoreType.DMA

    def body(states, mass, stiffness, scale, potential, slots, shared, coefficients):
        def run(*refs):
            kernel(parts, *refs)

        filtered = pl.pallas_call(
            run,
            out_shape=jax.ShapeDtypeStruct((OWN, BANDW), F32),
            in_specs=[hbm, hbm, hbm, smem, hbm, hbm, hbm, hbm],
            out_specs=vmem,
            scratch_shapes=[
                pltpu.VMEM(states.shape, F32),
                pltpu.VMEM(coefficients.shape, F32),
                pltpu.VMEM(shared.shape, jnp.int32),
                pltpu.VMEM(mass.shape, F32),
                pltpu.VMEM(stiffness.shape, F32),
                pltpu.VMEM(potential.shape, F32),
                pltpu.VMEM(slots.shape, jnp.int32),
                dma((7,)),
                pltpu.VMEM((PAD, PAD), F32),
                pltpu.VMEM((8, PAD), jnp.int32),
                pltpu.VMEM((8, PAD), F32),
                pltpu.VMEM((8, 256), jnp.int32),
                pltpu.VMEM((W, 896), F32),
                pltpu.VMEM((OWN, W), F32),
                pltpu.VMEM((OWN, W), F32),
                pltpu.VMEM((EDGE, W), F32),
                pltpu.VMEM((ROWS, CELLS * PAD), BF16),
                pltpu.VMEM((CELLS * PAD, OWN), BF16),
                pltpu.VMEM((CELLS * PAD, OWN), BF16),
                pltpu.VMEM((CELLS * PAD, 512), BF16),
                pltpu.VMEM((CELLS * PAD, 512), BF16),
                pltpu.VMEM((ROWS, OWN), BF16),
                pltpu.VMEM((ROWS, OWN), BF16),
                pltpu.VMEM((ROWS, 768), BF16),
                pltpu.VMEM((ROWS, 768), BF16),
                pltpu.VMEM((BOTH, OWN), BF16),
                pltpu.VMEM((2, OWN, EDGE), BF16),
                pltpu.VMEM((EDGE, EDGE), BF16),
                pltpu.VMEM((OWN, OWN), BF16),
                pltpu.VMEM((2, OWN, HALF), BF16),
                pltpu.VMEM((2, EDGE, W), F32),
                pltpu.VMEM((2, EDGE, W), F32),
                pltpu.VMEM((2, OWN, W), F32),
                pltpu.VMEM((2, OWN, W), F32),
                pltpu.VMEM((2, OWN, W), F32),
                pltpu.VMEM((2, OWN, W), F32),
                pltpu.VMEM((2, ROWS, W), F32),
                pltpu.VMEM((2, OWN, W), F32),
                pltpu.VMEM((2, 768, W), F32),
                pltpu.VMEM((2, 768, 2 * W), BF16),
                pltpu.VMEM((2, OWN, 2 * W), BF16),
                pltpu.VMEM((2, EDGE, W), F32),
                pltpu.VMEM((DEGREE, 2, BOTH, W), F32),
                pltpu.VMEM((DEGREE, 2, 2, EDGE, W), F32),
                pltpu.VMEM((DEGREE, 2, BOTH, W), F32),
                pltpu.VMEM((DEGREE, 2, 2, EDGE, W), F32),
                dma((2,)),
                dma((3,)),
                dma((3,)),
                dma((DEGREE, 2, 2)),
                dma((DEGREE, 2, 2)),
                dma((DEGREE, 2, 2)),
                dma((DEGREE, 2, 2)),
            ],
            compiler_params=pltpu.CompilerParams(
                collective_id=0, has_side_effects=True, vmem_limit_bytes=56 * 2**20
            ),
        )(states, mass, stiffness, scale, potential, slots, shared, coefficients)
        return filtered * COEFS[-1][0]

    return jax.shard_map(
        body,
        mesh=mesh,
        in_specs=(
            P("mesh", "band"),
            P("mesh"),
            P(),
            P("mesh"),
            P("mesh", None),
            P("mesh", None),
            P("mesh", None, None),
            P("band", None),
        ),
        out_specs=P("mesh", "band"),
        check_vma=False,
    )
```
